32 devices in a mesh: fsdp: 32 (over z, y, x, core).
Axes of the slice: x: 2, y: 2, z: 4, core: 2. Of those that a mesh axis runs over, the one named last changes fastest.
Arguments:
- tokens: bfloat16 [64, 64, 768], P('fsdp'), may hold values from -6 to 6
- segments: int32 [64, 64], P('fsdp'), may hold values from -1 to 3, as said below
- norm_gain: bfloat16 [2, 768], P(None, 'fsdp'), may hold values from 0.5 to 1.5
- in_weight: bfloat16 [2, 768, 3352], P(None, 'fsdp'), may hold values from -0.21875 to 0.21875
- conv_weight: bfloat16 [2, 4, 1792], P(None, None, 'fsdp'), may hold values from -3 to 3
- conv_bias: bfloat16 [2, 1792], P(None, 'fsdp'), may hold values from -3 to 3
- log_decay: float32 [2, 24], replicated, may hold values from 0 to 2.77
- skip_gain: float32 [2, 24], replicated, may hold values from 0.5 to 2
- step_bias: float32 [2, 24], replicated, may hold values from -6 to -1
- gate_gain: bfloat16 [2, 1536], P(None, 'fsdp'), may hold values from 0.5 to 1.5
- out_weight: bfloat16 [2, 1536, 768], P(None, 'fsdp'), may hold values from -0.15625 to 0.15625
- cotangent: bfloat16 [64, 64, 768], P('fsdp'), may hold values from -6 to 6
Outputs:
- mixed: bfloat16 [64, 64, 768], P('fsdp')
- token_grad: float32 [64, 64, 768], P('fsdp')
- norm_gain_grad: float32 [2, 768], P(None, 'fsdp')
- in_weight_grad: float32 [2, 768, 3352], P(None, 'fsdp')
- conv_weight_grad: float32 [2, 4, 1792], P(None, None, 'fsdp')
- conv_bias_grad: float32 [2, 1792], P(None, 'fsdp')
- log_decay_grad: float32 [2, 24], replicated
- skip_gain_grad: float32 [2, 24], replicated
- step_bias_grad: float32 [2, 24], replicated
- gate_gain_grad: float32 [2, 1536], P(None, 'fsdp')
- out_weight_grad: float32 [2, 1536, 768], P(None, 'fsdp')
The draws below stay inside these ranges and needn't reach their ends.
Inputs may be any that keep to these rules, and one draw needn't show every extreme that they name: `segments`: in each block the segment numbers start at 0 at the first position and never fall over the live positions; the positions after a block's live positions hold -1; each block has at least one live position.
All inputs are finite; a program needn't handle non-finite values.
Results may differ from the reference program's by a relative error of at most 0.012.
Values may be sent and summed in bfloat16 or wider, within the bound.
No kernel may reach another device: no remote copies, remote signals or barrier semaphores. Data moves between devices by JAX's collectives and lax.ppermute only.
A program may use at most 192 MiB of HBM per device.

```python
import jax
import jax.numpy as jnp
from jax import lax

D = 768
HEADS = 24
HEADDIM = 64
STATE = 128
CONV = 4
LAYERS = 2
BLOCK = 64
INNER = 1536
CONVCH = 1792
PROJ = 3352
BLOCKS = 64


def draw_segments(key, part):
    key = jax.random.fold_in(key, 11)
    keys = jax.random.split(key, 4)
    least = max(BLOCK // 8, 2)
    raw = jax.random.randint(keys[0], (BLOCKS,), 0, BLOCK + 1)
    live = jnp.maximum(least, raw * raw // BLOCK)
    count = jax.random.randint(keys[1], (BLOCKS,), 1, 5)
    picks = jax.random.randint(keys[2], (3,), 0, BLOCKS)
    index = jnp.arange(BLOCKS)
    live = jnp.where(index == picks[0], BLOCK, live)
    live = jnp.where(index == picks[1], least, live)
    count = jnp.where(index == picks[2], 4, count)
    cuts = jax.random.randint(keys[3], (BLOCKS, 3), 0, 1 << 20) % (live - 1)[:, None] + 1
    active = jnp.arange(3)[None, :] < (count - 1)[:, None]
    position = jnp.arange(BLOCK)
    passed = active[:, None, :] & (position[None, :, None] >= cuts[:, None, :])
    numbers = jnp.sum(passed.astype(jnp.int32), axis=2)
    numbers = jnp.where(position[None, :] < live[:, None], numbers, -1)
    return numbers.astype(jnp.int32)


def steps_of(rng, extent, shards, low, top_value):
    factor_of = 1.0
    for dim, blocks in shards:
        draws = jax.random.uniform(jax.random.fold_in(jax.random.fold_in(rng, 6), dim), (blocks,), jnp.float32, low / len(shards), top_value / len(shards))
        factor_of = factor_of * jnp.repeat(jnp.exp(draws), extent[dim] // blocks).reshape((-1,) + (1,) * (len(extent) - 1 - dim))
    return factor_of


def normal_values(stream_key, extent, deviation, limit, pieces=(), kind=jnp.bfloat16):
    array = jax.random.normal(stream_key, extent, jnp.float32) * deviation
    if len(pieces) > 0:
        array = steps_of(stream_key, extent, pieces, -0.22, 0.18) * array
    return jnp.clip(array, min=-limit, max=limit).astype(kind)


def setup_inputs(seed: int = 0) -> dict:
    seeds = jax.random.split(jax.random.key(seed), 13)
    return {
        "tokens": normal_values(seeds[0], (BLOCKS, BLOCK, D), 1.0, 6.0, ((0, 32),)),
        "segments": draw_segments(jax.random.fold_in(seeds[12], 71), 0),
        "norm_gain": jnp.clip(1.0 + 0.1 * jax.random.normal(seeds[2], (LAYERS, D), jnp.float32), 0.5, 1.5).astype(jnp.bfloat16),
        "in_weight": normal_values(seeds[3], (LAYERS, D, PROJ), D ** -0.5, 0.21875, ((1, 32),)),
        "conv_weight": normal_values(seeds[4], (LAYERS, CONV, CONVCH), CONV ** -0.5, 3.0, ((2, 32),)),
        "conv_bias": normal_values(seeds[5], (LAYERS, CONVCH), 0.5, 3.0, ((1, 32),)),
        "log_decay": jnp.clip(jax.random.uniform(seeds[6], (LAYERS, HEADS), jnp.float32, 0.0, 2.77), 0.0, 2.77),
        "skip_gain": jnp.clip(jax.random.uniform(seeds[7], (LAYERS, HEADS), jnp.float32, 0.5, 2.0), 0.5, 2.0),
        "step_bias": jnp.clip(jax.random.uniform(seeds[8], (LAYERS, HEADS), jnp.float32, -6.0, -1.0), -6.0, -1.0),
        "gate_gain": jnp.clip(1.0 + 0.1 * jax.random.normal(seeds[9], (LAYERS, INNER), jnp.float32), 0.5, 1.5).astype(jnp.bfloat16),
        "out_weight": normal_values(seeds[10], (LAYERS, INNER, D), INNER ** -0.5, 0.15625, ((1, 32),)),
        "cotangent": normal_values(seeds[11], (BLOCKS, BLOCK, D), 1.0, 6.0, ((0, 32),)),
    }


EPSILON = 1e-05
EXACT = lax.Precision.HIGHEST

@jax.custom_vjp
def low(v):
    return lax.optimization_barrier(v.astype(jnp.bfloat16)).astype(jnp.float32)

@jax.custom_vjp
def low_back(v):
    return v

def low_keep(v):
    return (low(v), None)

def low_pass(kept, grad):
    return (grad,)

def back_keep(v):
    return (v, None)

def back_low(kept, grad):
    return (low(grad),)
low.defvjp(low_keep, low_pass)
low_back.defvjp(back_keep, back_low)

def rms_norm(values, gain):
    return values * lax.rsqrt(lax.optimization_barrier(jnp.mean(values * values, axis=-1, keepdims=True)) + EPSILON) * gain

def segment_mixer(segment_ids, hidden, conv_weight, conv_bias, log_decay, skip_gain, step_bias, gate_gain):
    length = hidden.shape[0]
    inner = HEADS * HEADDIM
    gate_part = hidden[:, :inner]
    signal = hidden[:, inner:2 * inner + 2 * STATE]
    step_raw = hidden[:, 2 * inner + 2 * STATE:]
    mixed_conv = conv_bias + signal * conv_weight[CONV - 1]
    for offset in range(1, CONV):
        shifted = jnp.pad(signal, ((offset, 0), (0, 0)))[:length]
        earlier = jnp.pad(segment_ids, (offset, 0), constant_values=-2)[:length]
        mixed_conv = mixed_conv + jnp.where((earlier == segment_ids)[:, None], shifted, 0.0) * conv_weight[CONV - 1 - offset]
    mixed_conv = jax.nn.silu(mixed_conv)
    values = mixed_conv[:, :inner].reshape(length, HEADS, HEADDIM)
    inputs_b = mixed_conv[:, inner:inner + STATE]
    outputs_c = mixed_conv[:, inner + STATE:]
    step_size = jax.nn.softplus(step_raw + step_bias)
    rates = step_size * -jnp.exp(log_decay)
    totals = jnp.cumsum(rates, axis=0).T
    position = jnp.arange(length)
    allowed = (position[:, None] >= position[None, :]) & (segment_ids[:, None] == segment_ids[None, :])
    gaps = jnp.where(allowed[None], totals[:, :, None] - totals[:, None, :], 0.0)
    decays = jnp.where(allowed[None], jnp.exp(gaps), 0.0)
    scores = jnp.dot(outputs_c, inputs_b.T, precision=EXACT)
    weights = scores[None] * decays
    scaled = values * step_size[:, :, None]
    states = jnp.einsum('hts,shp->thp', weights, scaled, precision=EXACT)
    states = states + values * skip_gain[None, :, None]
    gated = states.reshape(length, inner) * jax.nn.silu(gate_part)
    return rms_norm(gated, gate_gain)

def layer(resid, segment_ids, params):
    norm_gain, in_weight, conv_weight, conv_bias, log_decay, skip_gain, step_bias, gate_gain, out_weight = params
    normed = low(rms_norm(resid, norm_gain))
    hidden = low_back(jnp.dot(normed, in_weight, precision=EXACT))
    gated = low(segment_mixer(segment_ids, hidden, conv_weight, conv_bias, log_decay, skip_gain, step_bias, gate_gain))
    return resid + low_back(jnp.dot(gated, out_weight, precision=EXACT))

def reference(tokens, segments, norm_gain, in_weight, conv_weight, conv_bias, log_decay, skip_gain, step_bias, gate_gain, out_weight, cotangent):
    weights = tuple((item.astype(jnp.float32) for item in (norm_gain, in_weight, conv_weight, conv_bias, log_decay, skip_gain, step_bias, gate_gain, out_weight)))
    resid = tokens.astype(jnp.float32)

    def run(resid, weights):

        def one_block(pair):
            block, segment_ids = pair
            for layer_index in range(LAYERS):
                block = layer(block, segment_ids, [item[layer_index] for item in weights])
            return block
        return lax.map(jax.checkpoint(one_block), (resid, segments))
    result, pull = jax.vjp(run, resid, weights)
    valid = (segments >= 0).astype(jnp.float32)[:, :, None]
    mixed = (result * valid).astype(jnp.bfloat16)
    token_grad, grads = pull(cotangent.astype(jnp.float32) * valid)
    return (mixed, token_grad, grads[0], grads[1], grads[2], grads[3], grads[4], grads[5], grads[6], grads[7], grads[8])
```

```python
from functools import partial

import jax
import jax.numpy as jnp
from jax import lax
from jax.experimental import pallas as pl
from jax.experimental.pallas import tpu as pltpu
from jax.sharding import PartitionSpec as P

HEADS = 24
HEADDIM = 64
STATE = 128
CONV = 4
BLOCK = 64
WIDTH = 768
INNER = HEADS * HEADDIM
CONVCH = INNER + 2 * STATE
PROJ = INNER + CONVCH + HEADS
LANES = 128
PADDED = INNER + CONVCH + LANES
PAIRS = INNER // LANES
STEP_AT = INNER + CONVCH
SMALL_ROWS = 8
PARTS = 32
EPSILON = 1e-05
EXACT = lax.Precision.HIGHEST
F32 = jnp.float32
LOW = jnp.bfloat16
NT = (((1,), (1,)), ((), ()))
TN = (((0,), (0,)), ((), ()))
VMEM_LIMIT = 56 * 1024 * 1024


def tile(index):
    return pl.ds(pl.multiple_of(index * LANES, LANES), LANES)


def iota(shape, dim):
    return lax.broadcasted_iota(jnp.int32, shape, dim)


def split(values):
    high = values.astype(LOW)
    return high, (values - high.astype(F32)).astype(LOW)


def low_half():
    return iota((1, LANES), 1) < HEADDIM


def set_masks(seg_col, seg_row, allowed_ref, taps_ref):
    rows = seg_col.shape[0]
    t, s = iota((rows, rows), 0), iota((rows, rows), 1)
    tri = (t >= s) & (t // BLOCK == s // BLOCK)
    allowed_ref[...] = jnp.where(tri & (seg_col == seg_row), 1.0, 0.0)
    wide = jnp.broadcast_to(seg_col, (rows, LANES))
    place = iota((rows, LANES), 0) % BLOCK
    for tap in range(1, CONV):
        earlier = pltpu.roll(wide, tap, axis=0)
        taps_ref[tap - 1] = jnp.where((earlier == wide) & (place >= tap), 1.0, 0.0)
    return jnp.where(tri, 1.0, 0.0)


def conv_tile(signal, weight_ref, bias_ref, taps_ref, at):
    total = bias_ref[:, at] + signal * weight_ref[CONV - 1 : CONV, at]
    for tap in range(1, CONV):
        shifted = pltpu.roll(signal, tap, axis=0) * taps_ref[tap - 1]
        total = total + shifted * weight_ref[CONV - 1 - tap : CONV - tap, at]
    return total


def steps(raw, heads_ref):
    raw = raw + heads_ref[2:3]
    step = jnp.maximum(raw, 0.0) + jnp.log1p(jnp.exp(-jnp.abs(raw)))
    return raw, step, step * -jnp.exp(heads_ref[0:1])


def spread_heads(high, low, index):
    head = iota((LANES, LANES), 0)
    lane = iota((LANES, LANES), 1)
    pick = jnp.where(head == 2 * index + lane // HEADDIM, 1.0, 0.0).astype(LOW)
    return jnp.dot(high, pick, preferred_element_type=F32) + jnp.dot(
        low, pick, preferred_element_type=F32
    )


def decays(turned_ref, allowed, head):
    rows = allowed.shape[0]
    across = jnp.broadcast_to(turned_ref[pl.ds(head, 1), :], (rows, rows))
    gaps = jnp.where(allowed > 0.0, across.T - across, -1e30)
    return jnp.exp(gaps)


def forward_kernel(
    resid_ref, in_ref, out_ref, norm_ref, conv_ref, bias_ref, gate_ref, heads_ref, skip_ref, col_ref, row_ref,
    next_ref, hidden_ref, mixed_ref, normed_ref, gated_ref,
    allowed_ref, taps_ref, turned_ref, scores_ref, product_ref,
):
    tri = set_masks(col_ref[...], row_ref[...], allowed_ref, taps_ref)
    resid = resid_ref[...]
    scale = lax.rsqrt(jnp.mean(resid * resid, axis=-1, keepdims=True) + EPSILON)
    normed_ref[...] = (resid * scale * norm_ref[...]).astype(LOW)

    def project(index, carry):
        at = pl.ds(pl.multiple_of(index * 3 * LANES, LANES), 3 * LANES)
        hidden_ref[:, at] = jnp.dot(normed_ref[...], in_ref[:, at], preferred_element_type=F32)
        return carry

    lax.fori_loop(0, PADDED // (3 * LANES), project, 0)
    raw, step, rate = steps(hidden_ref[:, STEP_AT:], heads_ref)
    turned_ref[...] = jnp.dot(tri, rate, precision=EXACT, preferred_element_type=F32).T
    high, low = split(step)
    pair = []
    for index in (0, 1):
        at = pl.ds(INNER + index * STATE, STATE)
        total = conv_tile(hidden_ref[:, pl.ds(2 * INNER + index * STATE, STATE)], conv_ref, bias_ref, taps_ref, at)
        pair.append(total * jax.nn.sigmoid(total))
    scores_ref[...] = lax.dot_general(pair[1], pair[0], NT, precision=EXACT, preferred_element_type=F32)
    first = low_half()

    def heads(index, squares):
        at = tile(index)
        total = conv_tile(hidden_ref[:, tile(index + PAIRS)], conv_ref, bias_ref, taps_ref, at)
        values = total * jax.nn.sigmoid(total)
        scaled = values * spread_heads(high, low, index)
        allowed = allowed_ref[...]
        scores = scores_ref[...]
        weights = jnp.concatenate(
            [(scores * decays(turned_ref, allowed, 2 * index + head)).astype(LOW) for head in (0, 1)], axis=1
        )
        both = jnp.concatenate([jnp.where(first, scaled, 0.0), jnp.where(first, 0.0, scaled)], axis=0).astype(LOW)
        mixed = jnp.dot(weights, both, preferred_element_type=F32)
        mixed_ref[:, at] = mixed
        gate = hidden_ref[:, at]
        product = (mixed + values * skip_ref[:, at]) * (gate * jax.nn.sigmoid(gate))
        product_ref[:, at] = product
        return squares + product * product

    squares = lax.fori_loop(0, PAIRS, heads, jnp.zeros((resid.shape[0], LANES), F32))
    scale = lax.rsqrt(jnp.sum(squares, axis=-1, keepdims=True) / INNER + EPSILON)
    gated_ref[...] = (product_ref[...] * scale * gate_ref[...]).astype(LOW)
    next_ref[...] = resid + jnp.dot(gated_ref[...], out_ref[...], preferred_element_type=F32)


def backward_kernel(
    me_ref, grad_ref, resid_ref, hidden_ref, mixed_ref, normed_ref, gated_ref,
    in_ref, out_ref, norm_ref, conv_ref, bias_ref, gate_ref, heads_ref, skip_ref, col_ref, row_ref,
    back_ref, in_keep_ref, in_send_ref, out_keep_ref, out_send_ref, small_ref,
    allowed_ref, taps_ref, turned_ref, scores_ref, dscores_ref, gated_grad_ref, values_ref, slope_ref,
    dhidden_ref, gathered_ref, turned_norm_ref, dnorm_ref,
):
    me = me_ref[0]
    core = me % 2
    chip = me // 2
    tri = set_masks(col_ref[...], row_ref[...], allowed_ref, taps_ref)
    rows = grad_ref.shape[0]
    grad_low = grad_ref[...].astype(LOW)
    small_ref[...] = jnp.zeros_like(small_ref)

    def out_back(index, carry):
        at = pl.ds(pl.multiple_of(index * 3 * LANES, LANES), 3 * LANES)
        gated_grad_ref[:, at] = lax.dot_general(grad_low, out_ref[at, :], NT, preferred_element_type=F32)
        part = lax.dot_general(gated_ref[:, at], grad_low, TN, preferred_element_type=F32)
        depth = INNER // PARTS
        for pair in range(3 * LANES // (2 * depth)):
            even = part[2 * pair * depth : (2 * pair + 1) * depth]
            odd = part[(2 * pair + 1) * depth : (2 * pair + 2) * depth]
            other = (index * (3 * LANES // (2 * depth)) + pair) ^ chip
            out_keep_ref[other % 4, other // 4] = jnp.where(core == 0, even, odd).astype(LOW)
            out_send_ref[other % 4, other // 4] = jnp.where(core == 0, odd, even).astype(LOW)
        return carry

    lax.fori_loop(0, INNER // (3 * LANES), out_back, 0)

    raw, step, rate = steps(hidden_ref[:, STEP_AT:], heads_ref)
    turned_ref[...] = jnp.dot(tri, rate, precision=EXACT, preferred_element_type=F32).T
    high, low = split(step)

    def again(index, carry):
        at = tile(index)
        total = conv_tile(hidden_ref[:, tile(index + PAIRS)], conv_ref, bias_ref, taps_ref, at)
        sigmoid = jax.nn.sigmoid(total)
        values_ref[:, at] = total * sigmoid
        slope_ref[:, at] = sigmoid * (1.0 + total * (1.0 - sigmoid))
        return carry

    lax.fori_loop(0, PAIRS + 2, again, 0)
    inputs_b = values_ref[:, INNER : INNER + STATE]
    outputs_c = values_ref[:, INNER + STATE :]
    scores_ref[...] = lax.dot_general(outputs_c, inputs_b, NT, precision=EXACT, preferred_element_type=F32)
    dscores_ref[...] = jnp.zeros_like(dscores_ref)

    def measure(index, carry):
        squares, dots = carry
        at = tile(index)
        gate = hidden_ref[:, at]
        product = (mixed_ref[:, at] + values_ref[:, at] * skip_ref[:, at]) * (gate * jax.nn.sigmoid(gate))
        return squares + product * product, dots + product * gated_grad_ref[:, at] * gate_ref[:, at]

    zero = jnp.zeros((rows, LANES), F32)
    squares, dots = lax.fori_loop(0, PAIRS, measure, (zero, zero))
    scale = lax.rsqrt(jnp.sum(squares, axis=-1, keepdims=True) / INNER + EPSILON)
    pull = scale * scale * scale * (jnp.sum(dots, axis=-1, keepdims=True) / INNER)
    first = low_half()

    def conv_back(index, du):
        at = tile(index)
        signal = hidden_ref[:, tile(index + PAIRS)]
        small_ref[5:6, at] = jnp.sum(du, axis=0, keepdims=True)
        small_ref[CONV : CONV + 1, at] = jnp.sum(du * signal, axis=0, keepdims=True)
        total = du * conv_ref[CONV - 1 : CONV, at]
        for tap in range(1, CONV):
            masked = du * taps_ref[tap - 1]
            shifted = pltpu.roll(signal, tap, axis=0)
            small_ref[CONV - tap : CONV - tap + 1, at] = jnp.sum(masked * shifted, axis=0, keepdims=True)
            total = total + pltpu.roll(masked, rows - tap, axis=0) * conv_ref[CONV - 1 - tap : CONV - tap, at]
        dhidden_ref[:, tile(index + PAIRS)] = total.astype(LOW)

    def heads(index, carry):
        dcum, dstep = carry
        at = tile(index)
        gate = hidden_ref[:, at]
        sigmoid = jax.nn.sigmoid(gate)
        silu = gate * sigmoid
        values = values_ref[:, at]
        mixed = mixed_ref[:, at]
        skip = skip_ref[:, at]
        states = mixed + values * skip
        product = states * silu
        gated_grad = gated_grad_ref[:, at]
        small_ref[6:7, at] = jnp.sum(gated_grad * product * scale, axis=0, keepdims=True)
        dproduct = scale * (gated_grad * gate_ref[:, at]) - product * pull
        dhidden_ref[:, at] = (dproduct * states * (sigmoid * (1.0 + gate * (1.0 - sigmoid)))).astype(LOW)
        dstates = dproduct * silu
        small_ref[7:8, at] = jnp.sum(dstates * values, axis=0, keepdims=True)
        step_wide = spread_heads(high, low, index)
        scaled = (values * step_wide).astype(LOW)
        dlow = dstates.astype(LOW)
        none = jnp.zeros_like(dlow)
        stacked = jnp.concatenate([jnp.where(first, dlow, none), jnp.where(first, none, dlow)], axis=0)
        allowed = allowed_ref[...]
        scores = scores_ref[...]
        factors = [decays(turned_ref, allowed, 2 * index + head) for head in (0, 1)]
        weights = jnp.concatenate([(scores * factor).astype(LOW) for factor in factors], axis=0)
        dweights = lax.dot_general(stacked, scaled, NT, preferred_element_type=F32)
        dscores_ref[...] += dweights[:rows] * factors[0] + dweights[rows:] * factors[1]
        dscaled = lax.dot_general(weights, stacked, TN, preferred_element_type=F32)
        head = iota((LANES, LANES), 1)
        lane = iota((LANES, LANES), 0)
        pick = jnp.where(head == 2 * index + lane // HEADDIM, 1.0, 0.0).astype(LOW)
        gained = split(dlow.astype(F32) * mixed - scaled.astype(F32) * dscaled)
        dcum = dcum + sum(jnp.dot(item, pick, preferred_element_type=F32) for item in gained)
        gained = split(values * dscaled)
        dstep = dstep + sum(jnp.dot(item, pick, preferred_element_type=F32) for item in gained)
        dvalues = step_wide * dscaled + skip * dstates
        conv_back(index, dvalues * slope_ref[:, at])
        return dcum, dstep

    dcum, dstep = lax.fori_loop(0, PAIRS, heads, (zero, zero))
    dscores = dscores_ref[...]
    dinputs = lax.dot_general(dscores, outputs_c, TN, precision=EXACT, preferred_element_type=F32)
    doutputs = jnp.dot(dscores, inputs_b, precision=EXACT, preferred_element_type=F32)
    conv_back(PAIRS, dinputs * slope_ref[:, INNER : INNER + STATE])
    conv_back(PAIRS + 1, doutputs * slope_ref[:, INNER + STATE :])
    drate = lax.dot_general(tri, dcum, TN, precision=EXACT, preferred_element_type=F32)
    small_ref[0:1, WIDTH : WIDTH + LANES] = jnp.sum(drate * rate, axis=0, keepdims=True)
    draw = (dstep - drate * jnp.exp(heads_ref[0:1])) * jax.nn.sigmoid(raw)
    small_ref[0:1, WIDTH + LANES : WIDTH + 2 * LANES] = jnp.sum(draw, axis=0, keepdims=True)
    dhidden_ref[:, STEP_AT:] = draw.astype(LOW)

    turned_norm_ref[...] = normed_ref[...].T
    dnorm_ref[...] = jnp.zeros_like(dnorm_ref)

    def in_back(index, carry):
        at = pl.ds(pl.multiple_of(index * 3 * LANES, LANES), 3 * LANES)
        dhidden = dhidden_ref[:, at]
        dnorm_ref[...] += lax.dot_general(dhidden, in_ref[:, at], NT, preferred_element_type=F32)
        gathered_ref[...] = jnp.dot(turned_norm_ref[...], dhidden, preferred_element_type=F32)
        depth = WIDTH // PARTS
        for pair in range(PARTS // 2):
            even = gathered_ref[2 * pair * depth : (2 * pair + 1) * depth]
            odd = gathered_ref[(2 * pair + 1) * depth : (2 * pair + 2) * depth]
            other = pair ^ chip
            in_keep_ref[other % 4, other // 4, :, at] = jnp.where(core == 0, even, odd).astype(LOW)
            in_send_ref[other % 4, other // 4, :, at] = jnp.where(core == 0, odd, even).astype(LOW)
        return carry

    lax.fori_loop(0, PADDED // (3 * LANES), in_back, 0)
    resid = resid_ref[...]
    scale = lax.rsqrt(jnp.mean(resid * resid, axis=-1, keepdims=True) + EPSILON)
    dnorm = dnorm_ref[...]
    small_ref[0:1, :WIDTH] = jnp.sum(dnorm * resid * scale, axis=0, keepdims=True)
    gained = dnorm * norm_ref[...]
    pull = scale * scale * scale * jnp.mean(gained * resid, axis=-1, keepdims=True)
    back_ref[...] = grad_ref[...] + scale * gained - resid * pull


def shape(*dims, dtype=F32):
    return jax.ShapeDtypeStruct(dims, dtype)


def mixer_scratch(rows):
    return [
        pltpu.VMEM((rows, rows), F32),
        pltpu.VMEM((CONV - 1, rows, LANES), F32),
        pltpu.VMEM((LANES, rows), F32),
        pltpu.VMEM((rows, rows), F32),
    ]


VMEM = pl.BlockSpec(memory_space=pltpu.VMEM)
SMEM = pl.BlockSpec(memory_space=pltpu.SMEM)


def forward(resid, weights, small, segs):
    rows = resid.shape[0]
    return pl.pallas_call(
        forward_kernel,
        out_shape=(
            shape(rows, WIDTH),
            shape(rows, PADDED),
            shape(rows, INNER),
            shape(rows, WIDTH, dtype=LOW),
            shape(rows, INNER, dtype=LOW),
        ),
        in_specs=[VMEM] * 11,
        out_specs=(VMEM,) * 5,
        scratch_shapes=mixer_scratch(rows) + [pltpu.VMEM((rows, INNER), F32)],
        compiler_params=pltpu.CompilerParams(vmem_limit_bytes=VMEM_LIMIT),
        cost_estimate=pl.CostEstimate(flops=40_000_000_000, bytes_accessed=12_000_000, transcendentals=0),
        name="block_forward",
    )(resid, *weights, *small, *segs)


def backward(me, grad, resid, kept, weights, small, segs):
    rows = resid.shape[0]
    in_part = shape(4, 4, WIDTH // PARTS, PADDED, dtype=LOW)
    out_part = shape(4, 4, INNER // PARTS, WIDTH, dtype=LOW)
    return pl.pallas_call(
        backward_kernel,
        out_shape=(shape(rows, WIDTH), in_part, in_part, out_part, out_part, shape(SMALL_ROWS, CONVCH)),
        in_specs=[SMEM] + [VMEM] * 16,
        out_specs=(VMEM,) * 6,
        scratch_shapes=mixer_scratch(rows)
        + [
            pltpu.VMEM((rows, rows), F32),
            pltpu.VMEM((rows, INNER), F32),
            pltpu.VMEM((rows, CONVCH), F32),
            pltpu.VMEM((rows, CONVCH), F32),
            pltpu.VMEM((rows, PADDED), LOW),
            pltpu.VMEM((WIDTH, 3 * LANES), F32),
            pltpu.VMEM((WIDTH, rows), LOW),
            pltpu.VMEM((rows, WIDTH), F32),
        ],
        compiler_params=pltpu.CompilerParams(vmem_limit_bytes=VMEM_LIMIT),
        cost_estimate=pl.CostEstimate(flops=60_000_000_000, bytes_accessed=24_000_000, transcendentals=0),
        name="block_backward",
    )(me, grad, resid, *kept, *weights, *small, *segs)


def swap(values, bit, count):
    return lax.ppermute(values, "fsdp", [(index, index ^ bit) for index in range(count)])


def place_kernel(me_ref, *refs):
    *pieces, whole_ref = refs
    me = me_ref[0]
    for core in (0, 1):
        cur, right, up, far_a, far_b = pieces[5 * core : 5 * core + 5]
        half = far_a.shape[0]
        for group, (ref, start) in enumerate(((cur, 0), (right, 0), (up, 0), (far_a, 0), (far_b, half))):
            for item in range(ref.shape[0]):
                away = 2 * (4 * (start + item) + min(group, 3)) + core
                whole_ref[me ^ away] = ref[item]


def gather(shard, me, count):
    if count != PARTS:
        return lax.all_gather(shard, "fsdp", axis=0, tiled=True)
    cur = shard[None]
    cur = jnp.concatenate([cur, swap(cur, 8, count)], axis=0)
    cur = jnp.concatenate([cur, swap(cur, 16, count)], axis=0)
    right, up = swap(cur, 2, count), swap(cur, 4, count)
    pieces = [cur, right, up, swap(right[:2], 4, count), swap(up[2:], 2, count)]
    pieces = pieces + [swap(piece, 1, count) for piece in pieces]
    whole = pl.pallas_call(
        place_kernel,
        out_shape=jax.ShapeDtypeStruct((PARTS,) + shard.shape, shard.dtype),
        in_specs=[SMEM] + [VMEM] * 10,
        out_specs=VMEM,
        compiler_params=pltpu.CompilerParams(vmem_limit_bytes=VMEM_LIMIT),
        cost_estimate=pl.CostEstimate(flops=0, bytes_accessed=10_000_000, transcendentals=0),
        name="place",
    )(me, *pieces)
    return whole.reshape(PARTS * shard.shape[0], shard.shape[1])


def scatter(keep, send, count):
    if count != PARTS:
        both = jnp.stack([jnp.swapaxes(keep, 0, 1), jnp.swapaxes(send, 0, 1)], axis=2)
        whole = both.reshape(-1, keep.shape[-1]).astype(F32)
        return lax.psum_scatter(whole, "fsdp", scatter_dimension=0, tiled=True)
    other = swap(send, 1, count)

    def local(group, low, high):
        return keep[group, low:high].astype(F32) + other[group, low:high].astype(F32)

    far_a = swap(local(3, 0, 2).astype(LOW), 4, count)
    far_b = swap(local(3, 2, 4).astype(LOW), 2, count)
    to_right = jnp.concatenate([local(1, 0, 2) + far_a.astype(F32), local(1, 2, 4)]).astype(LOW)
    to_up = jnp.concatenate([local(2, 0, 2), local(2, 2, 4) + far_b.astype(F32)]).astype(LOW)
    right, up = swap(to_right, 2, count), swap(to_up, 4, count)

    def mine(low, high):
        return local(0, low, high) + right[low:high].astype(F32) + up[low:high].astype(F32)

    deep = swap(mine(2, 4).astype(LOW), 16, count)
    near = swap((mine(1, 2) + deep[1:2].astype(F32)).astype(LOW), 8, count)
    return (mine(0, 1) + deep[0:1].astype(F32) + near.astype(F32))[0]


def gather_small(values, me, count):
    bit = 1
    while bit < count:
        other = swap(values, bit, count)
        upper = (me & bit) > 0
        values = jnp.where(
            upper, jnp.concatenate([other, values], axis=0), jnp.concatenate([values, other], axis=0)
        )
        bit *= 2
    return values


def sum_small(values, count):
    bit = 1
    while bit < count:
        values = values + swap(values, bit, count)
        bit *= 2
    return values


def body(
    count, tokens, segments, norm_gain, in_weight, conv_weight, conv_bias,
    log_decay, skip_gain, step_bias, gate_gain, out_weight, cotangent,
):
    layers, in_rows = in_weight.shape[:2]
    blocks = tokens.shape[0]
    rows = blocks * BLOCK
    me = lax.axis_index("fsdp")
    place = me if count == PARTS else me * 0
    place = place.astype(jnp.int32).reshape(1)
    chans = conv_bias.shape[1]
    widths = (in_rows, CONV * chans, chans, gate_gain.shape[1])
    packed = jnp.concatenate(
        [norm_gain, conv_weight.reshape(layers, -1), conv_bias, gate_gain], axis=1
    )
    packed = gather_small(packed[None], me, count)
    padded = jnp.pad(in_weight, ((0, 0), (0, 0), (0, PADDED - PROJ)))
    weights = [
        (gather(padded[layer], place, count), gather(out_weight[layer], place, count)) for layer in range(layers)
    ]
    small = []
    for layer in range(layers):
        ends = [sum(widths[: item + 1]) for item in range(4)]
        held = packed[:, layer].astype(F32)
        norm = held[:, : ends[0]].reshape(1, WIDTH)
        conv = held[:, ends[0] : ends[1]].reshape(count, CONV, chans)
        conv = jnp.swapaxes(conv, 0, 1).reshape(CONV, CONVCH)
        bias = held[:, ends[1] : ends[2]].reshape(1, CONVCH)
        gate = held[:, ends[2] :].reshape(1, INNER)
        heads = jnp.pad(
            jnp.stack([log_decay[layer], skip_gain[layer], step_bias[layer]]), ((0, 0), (0, LANES - HEADS))
        )
        skip = jnp.repeat(skip_gain[layer], HEADDIM).reshape(1, INNER)
        small.append((norm, conv, bias, gate, heads, skip))
    segs = (segments.reshape(rows, 1), segments.reshape(1, rows))
    resid = tokens.reshape(rows, WIDTH).astype(F32)
    kept = []
    for layer in range(layers):
        after, *saved = forward(resid, weights[layer], small[layer], segs)
        kept.append((resid, saved))
        resid = after
    valid = (segs[0] >= 0).astype(F32)
    mixed = (resid * valid).astype(LOW).reshape(tokens.shape)
    grad = cotangent.reshape(rows, WIDTH).astype(F32) * valid
    in_grads, out_grads, sums = [None] * layers, [None] * layers, [None] * layers
    for layer in reversed(range(layers)):
        resid, saved = kept[layer]
        grad, in_keep, in_send, out_keep, out_send, sums[layer] = backward(
            place, grad, resid, saved, weights[layer], small[layer], segs
        )
        out_grads[layer] = scatter(out_keep, out_send, count)
        in_grads[layer] = scatter(in_keep, in_send, count)[:, :PROJ]
    total = sum_small(jnp.stack(sums), count)

    def own(values, size):
        return lax.dynamic_slice_in_dim(values, me * size, size, axis=values.ndim - 1)

    by_head = total[:, 7, :INNER].reshape(layers, HEADS, HEADDIM).sum(axis=-1)
    return (
        mixed,
        grad.reshape(tokens.shape),
        own(total[:, 0, :WIDTH], in_rows),
        jnp.stack(in_grads),
        own(total[:, 1 : 1 + CONV], chans),
        own(total[:, 5], chans),
        total[:, 0, WIDTH : WIDTH + HEADS],
        by_head,
        total[:, 0, WIDTH + LANES : WIDTH + LANES + HEADS],
        own(total[:, 6, :INNER], gate_gain.shape[1]),
        jnp.stack(out_grads),
    )


def solution(mesh):
    split0 = P("fsdp", None, None)
    split1 = P(None, "fsdp", None)
    in_specs = (
        split0, P("fsdp", None), P(None, "fsdp"), split1, P(None, None, "fsdp"), P(None, "fsdp"),
        P(), P(), P(), P(None, "fsdp"), split1, split0,
    )
    out_specs = (
        split0, split0, P(None, "fsdp"), split1, P(None, None, "fsdp"), P(None, "fsdp"),
        P(), P(), P(), P(None, "fsdp"), split1,
    )
    return jax.shard_map(
        partial(body, mesh.shape["fsdp"]), mesh=mesh, in_specs=in_specs, out_specs=out_specs, check_vma=False
    )
```

```python
from functools import partial

import jax
import jax.numpy as jnp
from jax import lax
from jax.experimental import pallas as pl
from jax.experimental.pallas import tpu as pltpu
from jax.sharding import PartitionSpec as P

HEADS = 24
HEADDIM = 64
STATE = 128
CONV = 4
BLOCK = 64
WIDTH = 768
INNER = HEADS * HEADDIM
CONVCH = INNER + 2 * STATE
PROJ = INNER + CONVCH + HEADS
LANES = 128
PADDED = INNER + CONVCH + LANES
PAIRS = INNER // LANES
STEP_AT = INNER + CONVCH
SMALL_ROWS = 8
PARTS = 32
EPSILON = 1e-05
EXACT = lax.Precision.HIGHEST
F32 = jnp.float32
LOW = jnp.bfloat16
NT = (((1,), (1,)), ((), ()))
TN = (((0,), (0,)), ((), ()))
VMEM_LIMIT = 56 * 1024 * 1024


def tile(index):
    return pl.ds(pl.multiple_of(index * LANES, LANES), LANES)


def iota(shape, dim):
    return lax.broadcasted_iota(jnp.int32, shape, dim)


def split(values):
    high = values.astype(LOW)
    return high, (values - high.astype(F32)).astype(LOW)


def low_half():
    return iota((1, LANES), 1) < HEADDIM


def set_masks(seg_col, seg_row, allowed_ref, taps_ref):
    rows = seg_col.shape[0]
    t, s = iota((rows, rows), 0), iota((rows, rows), 1)
    tri = (t >= s) & (t // BLOCK == s // BLOCK)
    allowed_ref[...] = jnp.where(tri & (seg_col == seg_row), 1.0, 0.0)
    wide = jnp.broadcast_to(seg_col, (rows, LANES))
    place = iota((rows, LANES), 0) % BLOCK
    for tap in range(1, CONV):
        earlier = pltpu.roll(wide, tap, axis=0)
        taps_ref[tap - 1] = jnp.where((earlier == wide) & (place >= tap), 1.0, 0.0)
    return jnp.where(tri, 1.0, 0.0)


def conv_tile(signal, weight_ref, taps_ref, at):
    total = weight_ref[CONV : CONV + 1, at] + signal * weight_ref[CONV - 1 : CONV, at]
    for tap in range(1, CONV):
        shifted = pltpu.roll(signal, tap, axis=0) * taps_ref[tap - 1]
        total = total + shifted * weight_ref[CONV - 1 - tap : CONV - tap, at]
    return total


def steps(raw, heads_ref):
    raw = raw + heads_ref[2:3]
    step = jnp.maximum(raw, 0.0) + jnp.log1p(jnp.exp(-jnp.abs(raw)))
    return raw, step, step * -jnp.exp(heads_ref[0:1])


def spread_heads(high, low, index):
    head = iota((LANES, LANES), 0)
    lane = iota((LANES, LANES), 1)
    pick = jnp.where(head == 2 * index + lane // HEADDIM, 1.0, 0.0).astype(LOW)
    return jnp.dot(high, pick, preferred_element_type=F32) + jnp.dot(
        low, pick, preferred_element_type=F32
    )


def decays(turned_ref, allowed, head):
    rows = allowed.shape[0]
    across = jnp.broadcast_to(turned_ref[pl.ds(head, 1), :], (rows, rows))
    gaps = jnp.where(allowed > 0.0, across.T - across, -1e30)
    return jnp.exp(gaps)


def forward_kernel(
    resid_ref, in_ref, norm_ref, conv_ref, gate_ref, heads_ref, skip_ref, col_ref, row_ref,
    hidden_ref, mixed_ref, normed_ref, gated_ref,
    allowed_ref, taps_ref, turned_ref, scores_ref, product_ref,
):
    tri = set_masks(col_ref[...], row_ref[...], allowed_ref, taps_ref)
    resid = resid_ref[...]
    scale = lax.rsqrt(jnp.mean(resid * resid, axis=-1, keepdims=True) + EPSILON)
    normed_ref[...] = (resid * scale * norm_ref[...]).astype(LOW)

    def project(index, carry):
        at = pl.ds(pl.multiple_of(index * 3 * LANES, LANES), 3 * LANES)
        hidden_ref[:, at] = jnp.dot(normed_ref[...], in_ref[:, at], preferred_element_type=F32)
        return carry

    lax.fori_loop(0, PADDED // (3 * LANES), project, 0)
    raw, step, rate = steps(hidden_ref[:, STEP_AT:], heads_ref)
    turned_ref[...] = jnp.dot(tri, rate, precision=EXACT, preferred_element_type=F32).T
    high, low = split(step)
    pair = []
    for index in (0, 1):
        at = pl.ds(INNER + index * STATE, STATE)
        total = conv_tile(hidden_ref[:, pl.ds(2 * INNER + index * STATE, STATE)], conv_ref, taps_ref, at)
        pair.append(total * jax.nn.sigmoid(total))
    scores_ref[...] = lax.dot_general(pair[1], pair[0], NT, precision=EXACT, preferred_element_type=F32)
    first = low_half()

    def heads(index, squares):
        at = tile(index)
        total = conv_tile(hidden_ref[:, tile(index + PAIRS)], conv_ref, taps_ref, at)
        values = total * jax.nn.sigmoid(total)
        scaled = values * spread_heads(high, low, index)
        allowed = allowed_ref[...]
        scores = scores_ref[...]
        weights = jnp.concatenate(
            [(scores * decays(turned_ref, allowed, 2 * index + head)).astype(LOW) for head in (0, 1)], axis=1
        )
        both = jnp.concatenate([jnp.where(first, scaled, 0.0), jnp.where(first, 0.0, scaled)], axis=0).astype(LOW)
        mixed = jnp.dot(weights, both, preferred_element_type=F32)
        mixed_ref[:, at] = mixed
        gate = hidden_ref[:, at]
        product = (mixed + values * skip_ref[:, at]) * (gate * jax.nn.sigmoid(gate))
        product_ref[:, at] = product
        return squares + product * product

    squares = lax.fori_loop(0, PAIRS, heads, jnp.zeros((resid.shape[0], LANES), F32))
    scale = lax.rsqrt(jnp.sum(squares, axis=-1, keepdims=True) / INNER + EPSILON)
    gated_ref[...] = (product_ref[...] * scale * gate_ref[...]).astype(LOW)


def out_back(me_ref, grad_ref, gated_ref, out_ref, gated_grad_ref, store):
    core = me_ref[0] % 2
    chip = me_ref[0] // 2
    grad_low = grad_ref[...].astype(LOW)
    depth = INNER // PARTS
    pairs = 3 * LANES // (2 * depth)

    def step(index, carry):
        at = pl.ds(pl.multiple_of(index * 3 * LANES, LANES), 3 * LANES)
        gated_grad_ref[:, at] = lax.dot_general(grad_low, out_ref[at, :], NT, preferred_element_type=F32)
        part = lax.dot_general(gated_ref[:, at], grad_low, TN, preferred_element_type=F32)
        for pair in range(pairs):
            even = part[2 * pair * depth : (2 * pair + 1) * depth]
            odd = part[(2 * pair + 1) * depth : (2 * pair + 2) * depth]
            store((index * pairs + pair) ^ chip, jnp.where(core == 0, even, odd), jnp.where(core == 0, odd, even))
        return carry

    lax.fori_loop(0, INNER // (3 * LANES), step, 0)


def backward_out_kernel(me_ref, grad_ref, gated_ref, out_ref, gated_grad_ref, keep_ref, send_ref):
    def store(other, keep, send):
        keep_ref[other % 4, other // 4] = keep.astype(LOW)
        send_ref[other % 4, other // 4] = send.astype(LOW)

    out_back(me_ref, grad_ref, gated_ref, out_ref, gated_grad_ref, store)


def backward_mixer_kernel(
    gated_grad_ref, hidden_ref, mixed_ref, conv_ref, gate_ref, heads_ref, skip_ref, col_ref, row_ref,
    dhidden_ref, small_ref,
    allowed_ref, taps_ref, turned_ref, scores_ref, dscores_ref, values_ref, slope_ref,
):
    tri = set_masks(col_ref[...], row_ref[...], allowed_ref, taps_ref)
    rows = hidden_ref.shape[0]
    small_ref[...] = jnp.zeros_like(small_ref)
    raw, step, rate = steps(hidden_ref[:, STEP_AT:], heads_ref)
    turned_ref[...] = jnp.dot(tri, rate, precision=EXACT, preferred_element_type=F32).T
    high, low = split(step)

    def again(index, carry):
        at = tile(index)
        total = conv_tile(hidden_ref[:, tile(index + PAIRS)], conv_ref, taps_ref, at)
        sigmoid = jax.nn.sigmoid(total)
        values_ref[:, at] = total * sigmoid
        slope_ref[:, at] = sigmoid * (1.0 + total * (1.0 - sigmoid))
        return carry

    lax.fori_loop(0, PAIRS + 2, again, 0)
    inputs_b = values_ref[:, INNER : INNER + STATE]
    outputs_c = values_ref[:, INNER + STATE :]
    scores_ref[...] = lax.dot_general(outputs_c, inputs_b, NT, precision=EXACT, preferred_element_type=F32)
    dscores_ref[...] = jnp.zeros_like(dscores_ref)

    def measure(index, carry):
        squares, dots = carry
        at = tile(index)
        gate = hidden_ref[:, at]
        product = (mixed_ref[:, at] + values_ref[:, at] * skip_ref[:, at]) * (gate * jax.nn.sigmoid(gate))
        return squares + product * product, dots + product * gated_grad_ref[:, at] * gate_ref[:, at]

    zero = jnp.zeros((rows, LANES), F32)
    squares, dots = lax.fori_loop(0, PAIRS, measure, (zero, zero))
    scale = lax.rsqrt(jnp.sum(squares, axis=-1, keepdims=True) / INNER + EPSILON)
    pull = scale * scale * scale * (jnp.sum(dots, axis=-1, keepdims=True) / INNER)
    first = low_half()

    def conv_back(index, du):
        at = tile(index)
        signal = hidden_ref[:, tile(index + PAIRS)]
        small_ref[5:6, at] = jnp.sum(du, axis=0, keepdims=True)
        small_ref[CONV : CONV + 1, at] = jnp.sum(du * signal, axis=0, keepdims=True)
        total = du * conv_ref[CONV - 1 : CONV, at]
        for tap in range(1, CONV):
            masked = du * taps_ref[tap - 1]
            shifted = pltpu.roll(signal, tap, axis=0)
            small_ref[CONV - tap : CONV - tap + 1, at] = jnp.sum(masked * shifted, axis=0, keepdims=True)
            total = total + pltpu.roll(masked, rows - tap, axis=0) * conv_ref[CONV - 1 - tap : CONV - tap, at]
        dhidden_ref[:, tile(index + PAIRS)] = total.astype(LOW)

    def heads(index, carry):
        dcum, dstep = carry
        at = tile(index)
        gate = hidden_ref[:, at]
        sigmoid = jax.nn.sigmoid(gate)
        silu = gate * sigmoid
        values = values_ref[:, at]
        mixed = mixed_ref[:, at]
        skip = skip_ref[:, at]
        states = mixed + values * skip
        product = states * silu
        gated_grad = gated_grad_ref[:, at]
        small_ref[6:7, at] = jnp.sum(gated_grad * product * scale, axis=0, keepdims=True)
        dproduct = scale * (gated_grad * gate_ref[:, at]) - product * pull
        dhidden_ref[:, at] = (dproduct * states * (sigmoid * (1.0 + gate * (1.0 - sigmoid)))).astype(LOW)
        dstates = dproduct * silu
        small_ref[7:8, at] = jnp.sum(dstates * values, axis=0, keepdims=True)
        step_wide = spread_heads(high, low, index)
        scaled = (values * step_wide).astype(LOW)
        dlow = dstates.astype(LOW)
        none = jnp.zeros_like(dlow)
        stacked = jnp.concatenate([jnp.where(first, dlow, none), jnp.where(first, none, dlow)], axis=0)
        allowed = allowed_ref[...]
        scores = scores_ref[...]
        factors = [decays(turned_ref, allowed, 2 * index + head) for head in (0, 1)]
        weights = jnp.concatenate([(scores * factor).astype(LOW) for factor in factors], axis=0)
        dweights = lax.dot_general(stacked, scaled, NT, preferred_element_type=F32)
        dscores_ref[...] += dweights[:rows] * factors[0] + dweights[rows:] * factors[1]
        dscaled = lax.dot_general(weights, stacked, TN, preferred_element_type=F32)
        head = iota((LANES, LANES), 1)
        lane = iota((LANES, LANES), 0)
        pick = jnp.where(head == 2 * index + lane // HEADDIM, 1.0, 0.0).astype(LOW)
        gained = split(dlow.astype(F32) * mixed - scaled.astype(F32) * dscaled)
        dcum = dcum + sum(jnp.dot(item, pick, preferred_element_type=F32) for item in gained)
        gained = split(values * dscaled)
        dstep = dstep + sum(jnp.dot(item, pick, preferred_element_type=F32) for item in gained)
        dvalues = step_wide * dscaled + skip * dstates
        conv_back(index, dvalues * slope_ref[:, at])
        return dcum, dstep

    dcum, dstep = lax.fori_loop(0, PAIRS, heads, (zero, zero))
    dscores = dscores_ref[...]
    dinputs = lax.dot_general(dscores, outputs_c, TN, precision=EXACT, preferred_element_type=F32)
    doutputs = jnp.dot(dscores, inputs_b, precision=EXACT, preferred_element_type=F32)
    conv_back(PAIRS, dinputs * slope_ref[:, INNER : INNER + STATE])
    conv_back(PAIRS + 1, doutputs * slope_ref[:, INNER + STATE :])
    drate = lax.dot_general(tri, dcum, TN, precision=EXACT, preferred_element_type=F32)
    small_ref[0:1, :LANES] = jnp.sum(drate * rate, axis=0, keepdims=True)
    draw = (dstep - drate * jnp.exp(heads_ref[0:1])) * jax.nn.sigmoid(raw)
    small_ref[0:1, LANES : 2 * LANES] = jnp.sum(draw, axis=0, keepdims=True)
    dhidden_ref[:, STEP_AT:] = draw.astype(LOW)


def backward_in_kernel(
    me_ref, grad_ref, resid_ref, normed_ref, dhidden_ref, in_ref, norm_ref,
    back_ref, in_keep_ref, in_send_ref, norm_grad_ref,
    gathered_ref, turned_norm_ref, dnorm_ref, first=0,
):
    core = me_ref[0] % 2
    chip = me_ref[0] // 2
    turned_norm_ref[...] = normed_ref[...].T
    dnorm_ref[...] = jnp.zeros_like(dnorm_ref)

    def in_back(index, carry):
        at = pl.ds(pl.multiple_of(index * 3 * LANES, LANES), 3 * LANES)
        to = pl.ds(pl.multiple_of(first + index * 3 * LANES, LANES), 3 * LANES)
        dhidden = dhidden_ref[:, at]
        dnorm_ref[...] += lax.dot_general(dhidden, in_ref[:, at], NT, preferred_element_type=F32)
        gathered_ref[...] = jnp.dot(turned_norm_ref[...], dhidden, preferred_element_type=F32)
        depth = WIDTH // PARTS
        for pair in range(PARTS // 2):
            even = gathered_ref[2 * pair * depth : (2 * pair + 1) * depth]
            odd = gathered_ref[(2 * pair + 1) * depth : (2 * pair + 2) * depth]
            other = pair ^ chip
            in_keep_ref[other % 4, other // 4, :, to] = jnp.where(core == 0, even, odd).astype(LOW)
            in_send_ref[other % 4, other // 4, :, to] = jnp.where(core == 0, odd, even).astype(LOW)
        return carry

    lax.fori_loop(0, PADDED // (3 * LANES), in_back, 0)
    resid = resid_ref[...]
    scale = lax.rsqrt(jnp.mean(resid * resid, axis=-1, keepdims=True) + EPSILON)
    dnorm = dnorm_ref[...]
    norm_grad_ref[...] = jnp.sum(dnorm * resid * scale, axis=0, keepdims=True)
    gained = dnorm * norm_ref[...]
    pull = scale * scale * scale * jnp.mean(gained * resid, axis=-1, keepdims=True)
    back_ref[...] = grad_ref[...] + scale * gained - resid * pull


def backward_both_kernel(
    me_ref, grad_ref, resid_ref, normed_ref, dhidden_ref, in_ref, norm_ref, gated_ref, out_ref,
    back_ref, keep_ref, send_ref, norm_grad_ref, gated_grad_ref, *scratch,
):
    backward_in_kernel(
        me_ref, grad_ref, resid_ref, normed_ref, dhidden_ref, in_ref, norm_ref,
        back_ref, keep_ref, send_ref, norm_grad_ref, *scratch, first=2 * WIDTH,
    )
    depth = WIDTH // PARTS

    def store(other, keep, send):
        for half in (0, 1):
            at = pl.ds(half * WIDTH, WIDTH)
            rows = slice(half * depth, (half + 1) * depth)
            keep_ref[other % 4, other // 4, :, at] = keep[rows].astype(LOW)
            send_ref[other % 4, other // 4, :, at] = send[rows].astype(LOW)

    out_back(me_ref, back_ref, gated_ref, out_ref, gated_grad_ref, store)


def shape(*dims, dtype=F32):
    return jax.ShapeDtypeStruct(dims, dtype)


def mixer_scratch(rows):
    return [
        pltpu.VMEM((rows, rows), F32),
        pltpu.VMEM((CONV - 1, rows, LANES), F32),
        pltpu.VMEM((LANES, rows), F32),
        pltpu.VMEM((rows, rows), F32),
    ]


VMEM = pl.BlockSpec(memory_space=pltpu.VMEM)
SMEM = pl.BlockSpec(memory_space=pltpu.SMEM)


def call(kernel, name, flops, size, outs, scratch, *args):
    return pl.pallas_call(
        kernel,
        out_shape=outs,
        in_specs=[SMEM if item.shape == (1,) else VMEM for item in args],
        out_specs=(VMEM,) * len(outs),
        scratch_shapes=scratch,
        compiler_params=pltpu.CompilerParams(vmem_limit_bytes=VMEM_LIMIT),
        cost_estimate=pl.CostEstimate(flops=flops, bytes_accessed=size, transcendentals=0),
        name=name,
    )(*args)


def forward(resid, in_full, small, segs):
    rows = resid.shape[0]
    outs = (
        shape(rows, PADDED), shape(rows, INNER), shape(rows, WIDTH, dtype=LOW), shape(rows, INNER, dtype=LOW),
    )
    scratch = mixer_scratch(rows) + [pltpu.VMEM((rows, INNER), F32)]
    return call(
        forward_kernel, "mix_forward", 10_000_000_000, 10_000_000, outs, scratch, resid, in_full, *small, *segs
    )


def backward_out(me, grad, gated, out_full):
    part = shape(4, 4, INNER // PARTS, WIDTH, dtype=LOW)
    outs = (shape(grad.shape[0], INNER), part, part)
    return call(backward_out_kernel, "out_backward", 2_000_000_000, 8_000_000, outs, [], me, grad, gated, out_full)


def backward_mixer(gated_grad, hidden, mixed, small, segs):
    rows = hidden.shape[0]
    outs = (shape(rows, PADDED, dtype=LOW), shape(SMALL_ROWS, CONVCH))
    scratch = mixer_scratch(rows) + [
        pltpu.VMEM((rows, rows), F32), pltpu.VMEM((rows, CONVCH), F32), pltpu.VMEM((rows, CONVCH), F32),
    ]
    return call(
        backward_mixer_kernel, "mix_backward", 12_000_000_000, 5_000_000, outs, scratch,
        gated_grad, hidden, mixed, *small[1:], *segs,
    )


def backward_in(me, grad, resid, normed, dhidden, in_full, norm):
    rows = resid.shape[0]
    part = shape(4, 4, WIDTH // PARTS, PADDED, dtype=LOW)
    outs = (shape(rows, WIDTH), part, part, shape(1, WIDTH))
    scratch = [
        pltpu.VMEM((WIDTH, 3 * LANES), F32), pltpu.VMEM((WIDTH, rows), LOW), pltpu.VMEM((rows, WIDTH), F32),
    ]
    return call(
        backward_in_kernel, "in_backward", 6_000_000_000, 14_000_000, outs, scratch,
        me, grad, resid, normed, dhidden, in_full, norm,
    )


def backward_both(me, grad, resid, normed, dhidden, in_full, norm, gated, out_full):
    rows = resid.shape[0]
    part = shape(4, 4, WIDTH // PARTS, 2 * WIDTH + PADDED, dtype=LOW)
    outs = (shape(rows, WIDTH), part, part, shape(1, WIDTH), shape(rows, INNER))
    scratch = [
        pltpu.VMEM((WIDTH, 3 * LANES), F32), pltpu.VMEM((WIDTH, rows), LOW), pltpu.VMEM((rows, WIDTH), F32),
    ]
    return call(
        backward_both_kernel, "both_backward", 8_000_000_000, 22_000_000, outs, scratch,
        me, grad, resid, normed, dhidden, in_full, norm, gated, out_full,
    )


def swap(values, bit, count):
    return lax.ppermute(values, "fsdp", [(index, index ^ bit) for index in range(count)])


def place_kernel(cuts, me_ref, own_ref, other_ref, *whole_refs):
    me = me_ref[0]

    def step(item, carry):
        away = 2 * (4 * (item % 4) + item // 4)
        for core, ref in ((0, own_ref), (1, other_ref)):
            for starts, whole_ref in zip(cuts, whole_refs):
                for part, low in enumerate(starts):
                    high = low + whole_ref.shape[3]
                    whole_ref[me ^ (away + core), part] = ref[item, :, low:high]
        return carry

    lax.fori_loop(0, PARTS // 2, step, 0, unroll=4)


def phase(earlier, *items):
    held = lax.optimization_barrier(tuple(item[0] for item in items) + tuple(earlier))
    return [swap(value, item[1], PARTS) for value, item in zip(held, items)]


def after(earlier, *values):
    return lax.optimization_barrier(tuple(values) + tuple(earlier))[: len(values)]


def along_z(own):
    return [(own, 8), (own, 16), (own, 24)]


def along_xy(cur):
    return [(cur, 2), (cur, 4)]


def across(right, up):
    return [(right[:2], 4), (up[2:], 2)]


def join(own, others):
    return jnp.concatenate([own, *others], axis=0)


def put_together(me, own, other, *cuts):
    depth = own.shape[1]
    outs = tuple(shape(PARTS, len(starts), depth, width, dtype=LOW) for starts, width in cuts)
    kernel = partial(place_kernel, [starts for starts, width in cuts])
    wholes = call(kernel, "place", 0, 4 * own.size, outs, [], me, own, other)
    return [whole.reshape(-1, whole.shape[3]) for whole in wholes]


class Sums:
    def __init__(self, keep):
        self.keep = keep

    def add_core(self, other):
        self.other = other

    def local(self, group, low, high):
        return self.keep[group, low:high].astype(F32) + self.other[group, low:high].astype(F32)

    def across(self):
        return [(self.local(3, 0, 2).astype(LOW), 4), (self.local(3, 2, 4).astype(LOW), 2)]

    def along_xy(self, far_a, far_b):
        right = jnp.concatenate([self.local(1, 0, 2) + far_a.astype(F32), self.local(1, 2, 4)]).astype(LOW)
        up = jnp.concatenate([self.local(2, 0, 2), self.local(2, 2, 4) + far_b.astype(F32)]).astype(LOW)
        return [(right, 2), (up, 4)]

    def add_xy(self, right, up):
        self.mine = lambda low, high: (
            self.local(0, low, high) + right[low:high].astype(F32) + up[low:high].astype(F32)
        )

    def along_z(self):
        return [(self.mine(item, item + 1).astype(LOW), 8 * item) for item in (1, 2, 3)]

    def result(self, *parts):
        return sum([item.astype(F32) for item in parts], self.mine(0, 1))[0]

    def far_z(self):
        return [(self.mine(2, 4).astype(LOW), 16)]

    def near_z(self, far):
        self.far = far
        return [((self.mine(1, 2) + far[1:].astype(F32)).astype(LOW), 8)]

    def end(self, near):
        return self.result(self.far[:1], near)


def grow(values, other, me, bit):
    upper = (me & bit) > 0
    return jnp.where(upper, join(other, [values]), join(values, [other]))


def gather_small(values, me, count):
    bit = 1
    while bit < count:
        values = grow(values, swap(values, bit, count), me, bit)
        bit *= 2
    return values


def sum_small(values, count):
    bit = 1
    while bit < count:
        values = values + swap(values, bit, count)
        bit *= 2
    return values


def small_arrays(packed, count, widths, log_decay, skip_gain, step_bias):
    layers = packed.shape[1]
    norms, taps, gates = widths
    held = packed.astype(F32)

    def full(low, rows, width):
        part = held[:, :, low : low + rows * width].reshape(count, layers, rows, width)
        return jnp.transpose(part, (1, 2, 0, 3)).reshape(layers, rows, count * width)

    norm = full(0, 1, norms)
    conv = full(norms, CONV + 1, taps)
    gate = full(norms + (CONV + 1) * taps, 1, gates)
    heads = jnp.pad(jnp.stack([log_decay, skip_gain, step_bias], axis=1), ((0, 0), (0, 0), (0, LANES - HEADS)))
    skip = jnp.repeat(skip_gain, HEADDIM, axis=1)[:, None]
    return [[item[layer] for item in (norm, conv, gate, heads, skip)] for layer in range(layers)]


def project(resid, gated, out_full):
    return resid + jnp.dot(gated, out_full, preferred_element_type=F32)


def finish(resid, cotangent, segs):
    valid = (segs[0] >= 0).astype(F32)
    return (resid * valid).astype(LOW), cotangent.astype(F32) * valid


def run_plain(count, me, resid, segs, cotangent, in_shards, out_shards, packed, small_of):
    layers = len(in_shards)
    place = (me * 0).astype(jnp.int32).reshape(1)
    packed = gather_small(packed, me, count)
    small = small_of(packed)

    def whole(shard):
        return lax.all_gather(shard, "fsdp", axis=0, tiled=True)

    def scatter(keep, send):
        both = jnp.stack([jnp.swapaxes(keep, 0, 1), jnp.swapaxes(send, 0, 1)], axis=2)
        both = both.reshape(-1, keep.shape[-1]).astype(F32)
        return lax.psum_scatter(both, "fsdp", scatter_dimension=0, tiled=True)

    in_full = [whole(shard) for shard in in_shards]
    out_full = [whole(shard) for shard in out_shards]
    kept = []
    for layer in range(layers):
        saved = forward(resid, in_full[layer], small[layer], segs)
        kept.append((resid, saved))
        resid = project(resid, saved[3], out_full[layer])
    mixed, grad = finish(resid, cotangent, segs)
    in_grads, out_grads, sums, norm_sums = ([None] * layers for item in range(4))
    for layer in reversed(range(layers)):
        resid, (hidden, ssm, normed, gated) = kept[layer]
        gated_grad, out_keep, out_send = backward_out(place, grad, gated, out_full[layer])
        dhidden, sums[layer] = backward_mixer(gated_grad, hidden, ssm, small[layer], segs)
        grad, in_keep, in_send, norm_sums[layer] = backward_in(
            place, grad, resid, normed, dhidden, in_full[layer], small[layer][0]
        )
        out_grads[layer] = scatter(out_keep, out_send)
        in_grads[layer] = scatter(in_keep, in_send)
    sums = sum_small(jnp.stack(sums), count)
    norm_sums = sum_small(jnp.concatenate(norm_sums), count)
    return mixed, grad, in_grads, out_grads, sums, norm_sums


def run_staged(me, resid, segs, cotangent, in_shards, out_shards, packed, small_of):
    place = me.astype(jnp.int32).reshape(1)
    in0, in1 = (shard[None] for shard in in_shards)
    out0, out1 = (shard[None] for shard in out_shards)

    depth = in0.shape[1]
    second = jnp.concatenate([out0[:, :depth], out0[:, depth:], in1], axis=2)
    last = out1

    *got, other = phase([], *along_z(in0), (packed, 1))
    cur_a = join(in0, got)
    packed = grow(packed, other, me, 1)
    packed = grow(packed, swap(packed, 2, PARTS), me, 2)

    right_a, up_a, near, other = phase([cur_a, packed], *along_xy(cur_a), (second, 8), (packed, 4))
    cur_b = join(second, [near])
    packed = grow(packed, other, me, 4)

    *far_a, other = phase([right_a, up_a, cur_b, packed], *across(right_a, up_a), (packed, 8))
    (far_b,) = phase([right_a, up_a], (cur_b, 16))
    own_a = join(cur_a, [right_a, up_a, *far_a])
    packed = grow(packed, other, me, 8)

    other_a, near, other = phase([own_a, packed], (own_a, 1), (last, 8), (packed, 16))
    cur_b = join(cur_b, [far_b])
    cur_c = join(last, [near])
    packed = grow(packed, other, me, 16)
    small = small_of(packed)

    (in0_full,) = put_together(place, own_a, other_a, ((0,), PADDED))
    right_b, up_b, far_c = phase([in0_full, cur_c], *along_xy(cur_b), (cur_c, 16))
    kept0 = forward(*after([cur_b, *small[1]], resid), in0_full, small[0], segs)
    cur_c = join(cur_c, [far_c])

    far_b = phase([right_b, up_b, kept0[3]], *across(right_b, up_b))
    own_b = join(cur_b, [right_b, up_b, *far_b])
    other_b, right_c, up_c = phase([own_b, cur_c], (own_b, 1), *along_xy(cur_c))

    ready = [other_b]
    far_c = phase([other_b, right_c, up_c], *across(right_c, up_c))
    out0_full, in1_full = put_together(
        place, own_b, *after(ready, other_b), ((0, WIDTH), WIDTH), ((2 * WIDTH,), PADDED)
    )
    resid1 = project(resid, kept0[3], out0_full)
    own_c = join(cur_c, [right_c, up_c, *far_c])
    ready = [own_c, resid1]
    (other_c,) = phase(ready, (own_c, 1))
    kept1 = forward(*after(ready, resid1), in1_full, small[1], segs)
    (out1_full,) = put_together(place, own_c, *after([kept1[3]], other_c), ((0,), WIDTH))
    mixed, grad = finish(project(resid1, kept1[3], out1_full), cotangent, segs)

    hidden, ssm, normed, gated = kept1
    gated_grad, keep, send = backward_out(place, grad, gated, out1_full)
    sum_c = Sums(keep)
    (core,) = phase([gated_grad], (send, 1))
    dhidden, small1 = backward_mixer(gated_grad, hidden, ssm, small[1], segs)
    sum_c.add_core(core)

    ready = [core, dhidden]
    far_c = phase(ready, *sum_c.across())
    grad, keep, send, norm1, gated_grad = backward_both(
        place, grad, resid1, normed, *after(ready, dhidden), in1_full, small[1][0], kept0[3], out0_full
    )
    sum_b = Sums(keep)

    hidden, ssm, normed, gated = kept0
    ready = [*far_c, gated_grad]
    core, *got = phase(ready, (send, 1), *sum_c.along_xy(*far_c))
    dhidden, small0 = backward_mixer(*after(ready, gated_grad), hidden, ssm, small[0], segs)
    sums = jnp.stack([small0, small1])
    sum_b.add_core(core)
    sum_c.add_xy(*got)

    ready = [core, *got, dhidden]
    *far_b, far_c = phase(ready, *sum_b.across(), *sum_c.far_z())
    grad, keep, send, norm0 = backward_in(
        place, grad, resid, normed, *after(ready, dhidden), in0_full, small[0][0]
    )
    sum_a = Sums(keep)
    norms = jnp.stack([norm0, norm1])
    sums = jnp.concatenate([jnp.concatenate([sums[:, :1, : 2 * LANES], norms, sums[:, :1, 2 * LANES + WIDTH :]], axis=2), sums[:, 1:]], axis=1)

    ready = [*far_b, far_c, grad]
    core, near_c, right_b, up_b = phase(ready, (send, 1), *sum_c.near_z(far_c), *sum_b.along_xy(*far_b))
    sum_a.add_core(core)
    sum_b.add_xy(right_b, up_b)

    far_a = phase([core, near_c], *sum_a.across())
    sums += swap(*after(far_a, sums), 1, PARTS)
    ready = [*far_a, right_b, up_b, sums]
    right_a, up_a, far_b, other = phase(ready, *sum_a.along_xy(*far_a), *sum_b.far_z(), (sums, 2))
    sums += other
    sums += swap(sums, 4, PARTS)
    sums += swap(sums, 8, PARTS)
    sum_a.add_xy(right_a, up_a)

    *parts, near_b = phase([right_a, up_a, far_b, sums], *sum_a.along_z(), *sum_b.near_z(far_b))
    sums += swap(*after([near_b], sums), 16, PARTS)
    both = sum_b.end(near_b)
    in_grads = [sum_a.result(*parts), both[:, 2 * WIDTH :]]
    out_grads = [jnp.concatenate([both[:, :WIDTH], both[:, WIDTH : 2 * WIDTH]]), sum_c.end(near_c)]
    return mixed, grad, in_grads, out_grads, sums, sums[:, 0, 2 * LANES : 2 * LANES + WIDTH]


def body(
    count, tokens, segments, norm_gain, in_weight, conv_weight, conv_bias,
    log_decay, skip_gain, step_bias, gate_gain, out_weight, cotangent,
):
    layers, in_rows = in_weight.shape[:2]
    rows = tokens.shape[0] * BLOCK
    me = lax.axis_index("fsdp")
    chans, gates = conv_bias.shape[1], gate_gain.shape[1]
    packed = jnp.concatenate([norm_gain, conv_weight.reshape(layers, -1), conv_bias, gate_gain], axis=1)[None]
    padded = jnp.pad(in_weight, ((0, 0), (0, 0), (0, PADDED - PROJ)))
    segs = (segments.reshape(rows, 1), segments.reshape(1, rows))

    def small_of(packed):
        return small_arrays(packed, count, (in_rows, chans, gates), log_decay, skip_gain, step_bias)

    run = run_staged if count == PARTS and layers == 2 else partial(run_plain, count)
    mixed, grad, in_grads, out_grads, sums, norms = run(
        me, tokens.reshape(rows, WIDTH).astype(F32), segs, cotangent.reshape(rows, WIDTH),
        [padded[layer] for layer in range(layers)], [out_weight[layer] for layer in range(layers)], packed, small_of,
    )
    total = sums

    def own(values, size):
        return lax.dynamic_slice_in_dim(values, me * size, size, axis=values.ndim - 1)

    by_head = total[:, 7, :INNER].reshape(layers, HEADS, HEADDIM).sum(axis=-1)
    return (
        mixed.reshape(tokens.shape),
        grad.reshape(tokens.shape),
        own(norms, in_rows),
        jnp.stack([item[:, :PROJ] for item in in_grads]),
        own(total[:, 1 : 1 + CONV], chans),
        own(total[:, 5], chans),
        total[:, 0, :HEADS],
        by_head,
        total[:, 0, LANES : LANES + HEADS],
        own(total[:, 6, :INNER], gates),
        jnp.stack(out_grads),
    )


def solution(mesh):
    split0 = P("fsdp", None, None)
    split1 = P(None, "fsdp", None)
    in_specs = (
        split0, P("fsdp", None), P(None, "fsdp"), split1, P(None, None, "fsdp"), P(None, "fsdp"),
        P(), P(), P(), P(None, "fsdp"), split1, split0,
    )
    out_specs = (
        split0, split0, P(None, "fsdp"), split1, P(None, None, "fsdp"), P(None, "fsdp"),
        P(), P(), P(), P(None, "fsdp"), split1,
    )
    return jax.shard_map(
        partial(body, mesh.shape["fsdp"]), mesh=mesh, in_specs=in_specs, out_specs=out_specs, check_vma=False
    )
```

```python
from functools import partial

import jax
import jax.numpy as jnp
from jax import lax
from jax.experimental import pallas as pl
from jax.experimental.pallas import tpu as pltpu
from jax.sharding import PartitionSpec as P

HEADS = 24
HEADDIM = 64
STATE = 128
CONV = 4
BLOCK = 64
WIDTH = 768
INNER = HEADS * HEADDIM
CONVCH = INNER + 2 * STATE
PROJ = INNER + CONVCH + HEADS
LANES = 128
PADDED = INNER + CONVCH + LANES
PAIRS = INNER // LANES
STEP_AT = INNER + CONVCH
SMALL_ROWS = 8
PARTS = 32
EPSILON = 1e-05
EXACT = lax.Precision.HIGHEST
F32 = jnp.float32
LOW = jnp.bfloat16
NT = (((1,), (1,)), ((), ()))
TN = (((0,), (0,)), ((), ()))
VMEM_LIMIT = 56 * 1024 * 1024


def tile(index):
    return pl.ds(pl.multiple_of(index * LANES, LANES), LANES)


def iota(shape, dim):
    return lax.broadcasted_iota(jnp.int32, shape, dim)


def split(values):
    high = values.astype(LOW)
    return high, (values - high.astype(F32)).astype(LOW)


def low_half():
    return iota((1, LANES), 1) < HEADDIM


def set_masks(seg_col, seg_row, allowed_ref, taps_ref):
    rows = seg_col.shape[0]
    t, s = iota((rows, rows), 0), iota((rows, rows), 1)
    tri = (t >= s) & (t // BLOCK == s // BLOCK)
    allowed_ref[...] = jnp.where(tri & (seg_col == seg_row), 1.0, 0.0)
    wide = jnp.broadcast_to(seg_col, (rows, LANES))
    place = iota((rows, LANES), 0) % BLOCK
    for tap in range(1, CONV):
        earlier = pltpu.roll(wide, tap, axis=0)
        taps_ref[tap - 1] = jnp.where((earlier == wide) & (place >= tap), 1.0, 0.0)
    return jnp.where(tri, 1.0, 0.0)


def conv_tile(signal, weight_ref, taps_ref, at):
    total = weight_ref[CONV : CONV + 1, at] + signal * weight_ref[CONV - 1 : CONV, at]
    for tap in range(1, CONV):
        shifted = pltpu.roll(signal, tap, axis=0) * taps_ref[tap - 1]
        total = total + shifted * weight_ref[CONV - 1 - tap : CONV - tap, at]
    return total


def steps(raw, heads_ref):
    raw = raw + heads_ref[2:3]
    step = jnp.maximum(raw, 0.0) + jnp.log1p(jnp.exp(-jnp.abs(raw)))
    return raw, step, step * -jnp.exp(heads_ref[0:1])


def spread_heads(high, low, index):
    head = iota((LANES, LANES), 0)
    lane = iota((LANES, LANES), 1)
    pick = jnp.where(head == 2 * index + lane // HEADDIM, 1.0, 0.0).astype(LOW)
    return jnp.dot(high, pick, preferred_element_type=F32) + jnp.dot(
        low, pick, preferred_element_type=F32
    )


def decays(turned_ref, allowed, head):
    rows = allowed.shape[0]
    across = jnp.broadcast_to(turned_ref[pl.ds(head, 1), :], (rows, rows))
    gaps = jnp.where(allowed > 0.0, across.T - across, -1e30)
    return jnp.exp(gaps)


def forward_kernel(
    resid_ref, in_ref, norm_ref, conv_ref, gate_ref, heads_ref, skip_ref, col_ref, row_ref,
    hidden_ref, mixed_ref, normed_ref, gated_ref,
    allowed_ref, taps_ref, turned_ref, scores_ref, product_ref,
):
    tri = set_masks(col_ref[...], row_ref[...], allowed_ref, taps_ref)
    resid = resid_ref[...]
    scale = lax.rsqrt(jnp.mean(resid * resid, axis=-1, keepdims=True) + EPSILON)
    normed_ref[...] = (resid * scale * norm_ref[...]).astype(LOW)

    def project(index, carry):
        at = pl.ds(pl.multiple_of(index * 3 * LANES, LANES), 3 * LANES)
        hidden_ref[:, at] = jnp.dot(normed_ref[...], in_ref[:, at], preferred_element_type=F32)
        return carry

    lax.fori_loop(0, PADDED // (3 * LANES), project, 0)
    raw, step, rate = steps(hidden_ref[:, STEP_AT:], heads_ref)
    turned_ref[...] = jnp.dot(tri, rate, precision=EXACT, preferred_element_type=F32).T
    high, low = split(step)
    pair = []
    for index in (0, 1):
        at = pl.ds(INNER + index * STATE, STATE)
        total = conv_tile(hidden_ref[:, pl.ds(2 * INNER + index * STATE, STATE)], conv_ref, taps_ref, at)
        pair.append(total * jax.nn.sigmoid(total))
    scores_ref[...] = lax.dot_general(pair[1], pair[0], NT, precision=EXACT, preferred_element_type=F32)
    first = low_half()

    def heads(index, squares):
        at = tile(index)
        total = conv_tile(hidden_ref[:, tile(index + PAIRS)], conv_ref, taps_ref, at)
        values = total * jax.nn.sigmoid(total)
        scaled = values * spread_heads(high, low, index)
        allowed = allowed_ref[...]
        scores = scores_ref[...]
        weights = jnp.concatenate(
            [(scores * decays(turned_ref, allowed, 2 * index + head)).astype(LOW) for head in (0, 1)], axis=1
        )
        both = jnp.concatenate([jnp.where(first, scaled, 0.0), jnp.where(first, 0.0, scaled)], axis=0).astype(LOW)
        mixed = jnp.dot(weights, both, preferred_element_type=F32)
        mixed_ref[:, at] = mixed
        gate = hidden_ref[:, at]
        product = (mixed + values * skip_ref[:, at]) * (gate * jax.nn.sigmoid(gate))
        product_ref[:, at] = product
        return squares + product * product

    squares = lax.fori_loop(0, PAIRS, heads, jnp.zeros((resid.shape[0], LANES), F32))
    scale = lax.rsqrt(jnp.sum(squares, axis=-1, keepdims=True) / INNER + EPSILON)
    gated_ref[...] = (product_ref[...] * scale * gate_ref[...]).astype(LOW)


def out_back(me_ref, grad_ref, gated_ref, out_ref, gated_grad_ref, store):
    core = me_ref[0] % 2
    chip = me_ref[0] // 2
    grad_low = grad_ref[...].astype(LOW)
    depth = INNER // PARTS
    pairs = 3 * LANES // (2 * depth)

    def step(index, carry):
        at = pl.ds(pl.multiple_of(index * 3 * LANES, LANES), 3 * LANES)
        gated_grad_ref[:, at] = lax.dot_general(grad_low, out_ref[at, :], NT, preferred_element_type=F32)
        part = lax.dot_general(gated_ref[:, at], grad_low, TN, preferred_element_type=F32)
        for pair in range(pairs):
            even = part[2 * pair * depth : (2 * pair + 1) * depth]
            odd = part[(2 * pair + 1) * depth : (2 * pair + 2) * depth]
            store((index * pairs + pair) ^ chip, jnp.where(core == 0, even, odd), jnp.where(core == 0, odd, even))
        return carry

    lax.fori_loop(0, INNER // (3 * LANES), step, 0)


def backward_out_kernel(me_ref, grad_ref, gated_ref, out_ref, gated_grad_ref, keep_ref, send_ref):
    def store(other, keep, send):
        keep_ref[other % 4, other // 4] = keep.astype(LOW)
        send_ref[other % 4, other // 4] = send.astype(LOW)

    out_back(me_ref, grad_ref, gated_ref, out_ref, gated_grad_ref, store)


def backward_mixer_kernel(
    gated_grad_ref, hidden_ref, mixed_ref, conv_ref, gate_ref, heads_ref, skip_ref, col_ref, row_ref,
    dhidden_ref, small_ref,
    allowed_ref, taps_ref, turned_ref, scores_ref, dscores_ref, values_ref, slope_ref,
):
    tri = set_masks(col_ref[...], row_ref[...], allowed_ref, taps_ref)
    rows = hidden_ref.shape[0]
    small_ref[...] = jnp.zeros_like(small_ref)
    raw, step, rate = steps(hidden_ref[:, STEP_AT:], heads_ref)
    turned_ref[...] = jnp.dot(tri, rate, precision=EXACT, preferred_element_type=F32).T
    high, low = split(step)

    def again(index, carry):
        at = tile(index)
        total = conv_tile(hidden_ref[:, tile(index + PAIRS)], conv_ref, taps_ref, at)
        sigmoid = jax.nn.sigmoid(total)
        values_ref[:, at] = total * sigmoid
        slope_ref[:, at] = sigmoid * (1.0 + total * (1.0 - sigmoid))
        return carry

    lax.fori_loop(0, PAIRS + 2, again, 0)
    inputs_b = values_ref[:, INNER : INNER + STATE]
    outputs_c = values_ref[:, INNER + STATE :]
    scores_ref[...] = lax.dot_general(outputs_c, inputs_b, NT, precision=EXACT, preferred_element_type=F32)
    dscores_ref[...] = jnp.zeros_like(dscores_ref)

    def measure(index, carry):
        squares, dots = carry
        at = tile(index)
        gate = hidden_ref[:, at]
        product = (mixed_ref[:, at] + values_ref[:, at] * skip_ref[:, at]) * (gate * jax.nn.sigmoid(gate))
        return squares + product * product, dots + product * gated_grad_ref[:, at] * gate_ref[:, at]

    zero = jnp.zeros((rows, LANES), F32)
    squares, dots = lax.fori_loop(0, PAIRS, measure, (zero, zero))
    scale = lax.rsqrt(jnp.sum(squares, axis=-1, keepdims=True) / INNER + EPSILON)
    pull = scale * scale * scale * (jnp.sum(dots, axis=-1, keepdims=True) / INNER)
    first = low_half()

    def conv_back(index, du):
        at = tile(index)
        signal = hidden_ref[:, tile(index + PAIRS)]
        small_ref[5:6, at] = jnp.sum(du, axis=0, keepdims=True)
        small_ref[CONV : CONV + 1, at] = jnp.sum(du * signal, axis=0, keepdims=True)
        total = du * conv_ref[CONV - 1 : CONV, at]
        for tap in range(1, CONV):
            masked = du * taps_ref[tap - 1]
            shifted = pltpu.roll(signal, tap, axis=0)
            small_ref[CONV - tap : CONV - tap + 1, at] = jnp.sum(masked * shifted, axis=0, keepdims=True)
            total = total + pltpu.roll(masked, rows - tap, axis=0) * conv_ref[CONV - 1 - tap : CONV - tap, at]
        dhidden_ref[:, tile(index + PAIRS)] = total.astype(LOW)

    def heads(index, carry):
        dcum, dstep = carry
        at = tile(index)
        gate = hidden_ref[:, at]
        sigmoid = jax.nn.sigmoid(gate)
        silu = gate * sigmoid
        values = values_ref[:, at]
        mixed = mixed_ref[:, at]
        skip = skip_ref[:, at]
        states = mixed + values * skip
        product = states * silu
        gated_grad = gated_grad_ref[:, at]
        small_ref[6:7, at] = jnp.sum(gated_grad * product * scale, axis=0, keepdims=True)
        dproduct = scale * (gated_grad * gate_ref[:, at]) - product * pull
        dhidden_ref[:, at] = (dproduct * states * (sigmoid * (1.0 + gate * (1.0 - sigmoid)))).astype(LOW)
        dstates = dproduct * silu
        small_ref[7:8, at] = jnp.sum(dstates * values, axis=0, keepdims=True)
        step_wide = spread_heads(high, low, index)
        scaled = (values * step_wide).astype(LOW)
        dlow = dstates.astype(LOW)
        none = jnp.zeros_like(dlow)
        stacked = jnp.concatenate([jnp.where(first, dlow, none), jnp.where(first, none, dlow)], axis=0)
        allowed = allowed_ref[...]
        scores = scores_ref[...]
        factors = [decays(turned_ref, allowed, 2 * index + head) for head in (0, 1)]
        weights = jnp.concatenate([(scores * factor).astype(LOW) for factor in factors], axis=0)
        dweights = lax.dot_general(stacked, scaled, NT, preferred_element_type=F32)
        dscores_ref[...] += dweights[:rows] * factors[0] + dweights[rows:] * factors[1]
        dscaled = lax.dot_general(weights, stacked, TN, preferred_element_type=F32)
        head = iota((LANES, LANES), 1)
        lane = iota((LANES, LANES), 0)
        pick = jnp.where(head == 2 * index + lane // HEADDIM, 1.0, 0.0).astype(LOW)
        gained = split(dlow.astype(F32) * mixed - scaled.astype(F32) * dscaled)
        dcum = dcum + sum(jnp.dot(item, pick, preferred_element_type=F32) for item in gained)
        gained = split(values * dscaled)
        dstep = dstep + sum(jnp.dot(item, pick, preferred_element_type=F32) for item in gained)
        dvalues = step_wide * dscaled + skip * dstates
        conv_back(index, dvalues * slope_ref[:, at])
        return dcum, dstep

    dcum, dstep = lax.fori_loop(0, PAIRS, heads, (zero, zero))
    dscores = dscores_ref[...]
    dinputs = lax.dot_general(dscores, outputs_c, TN, precision=EXACT, preferred_element_type=F32)
    doutputs = jnp.dot(dscores, inputs_b, precision=EXACT, preferred_element_type=F32)
    conv_back(PAIRS, dinputs * slope_ref[:, INNER : INNER + STATE])
    conv_back(PAIRS + 1, doutputs * slope_ref[:, INNER + STATE :])
    drate = lax.dot_general(tri, dcum, TN, precision=EXACT, preferred_element_type=F32)
    small_ref[0:1, :LANES] = jnp.sum(drate * rate, axis=0, keepdims=True)
    draw = (dstep - drate * jnp.exp(heads_ref[0:1])) * jax.nn.sigmoid(raw)
    small_ref[0:1, LANES : 2 * LANES] = jnp.sum(draw, axis=0, keepdims=True)
    dhidden_ref[:, STEP_AT:] = draw.astype(LOW)


def backward_in_kernel(
    me_ref, grad_ref, resid_ref, normed_ref, dhidden_ref, in_ref, norm_ref,
    back_ref, in_keep_ref, in_send_ref,
    gathered_ref, turned_norm_ref, dnorm_ref, first=0,
):
    core = me_ref[0] % 2
    chip = me_ref[0] // 2
    turned_norm_ref[...] = normed_ref[...].T
    dnorm_ref[...] = jnp.zeros_like(dnorm_ref)

    def in_back(index, carry):
        at = pl.ds(pl.multiple_of(index * 3 * LANES, LANES), 3 * LANES)
        to = pl.ds(pl.multiple_of(first + index * 3 * LANES, LANES), 3 * LANES)
        dhidden = dhidden_ref[:, at]
        dnorm_ref[...] += lax.dot_general(dhidden, in_ref[:, at], NT, preferred_element_type=F32)
        gathered_ref[...] = jnp.dot(turned_norm_ref[...], dhidden, preferred_element_type=F32)
        store(slice(None), to)
        return carry

    def store(part, to):
        depth = WIDTH // PARTS
        for pair in range(PARTS // 2):
            even = gathered_ref[2 * pair * depth : (2 * pair + 1) * depth, part]
            odd = gathered_ref[(2 * pair + 1) * depth : (2 * pair + 2) * depth, part]
            other = pair ^ chip
            in_keep_ref[other % 4, other // 4, :, to] = jnp.where(core == 0, even, odd).astype(LOW)
            in_send_ref[other % 4, other // 4, :, to] = jnp.where(core == 0, odd, even).astype(LOW)

    lax.fori_loop(0, PADDED // (3 * LANES), in_back, 0)
    resid = resid_ref[...]
    scale = lax.rsqrt(jnp.mean(resid * resid, axis=-1, keepdims=True) + EPSILON)
    dnorm = dnorm_ref[...]
    norm_grad = jnp.sum(dnorm * resid * scale, axis=0, keepdims=True)
    column = jnp.broadcast_to(norm_grad, (LANES, WIDTH)).T
    spare = iota((1, LANES), 1) == HEADS
    gathered_ref[:, 2 * LANES :] = jnp.where(spare, column, gathered_ref[:, 2 * LANES :])
    store(slice(2 * LANES, 3 * LANES), pl.ds(first + STEP_AT, LANES))
    gained = dnorm * norm_ref[...]
    pull = scale * scale * scale * jnp.mean(gained * resid, axis=-1, keepdims=True)
    back_ref[...] = grad_ref[...] + scale * gained - resid * pull


def backward_both_kernel(
    me_ref, grad_ref, resid_ref, normed_ref, dhidden_ref, in_ref, norm_ref, gated_ref, out_ref,
    back_ref, keep_ref, send_ref, gated_grad_ref, *scratch,
):
    backward_in_kernel(
        me_ref, grad_ref, resid_ref, normed_ref, dhidden_ref, in_ref, norm_ref,
        back_ref, keep_ref, send_ref, *scratch, first=2 * WIDTH,
    )
    depth = WIDTH // PARTS

    def store(other, keep, send):
        for half in (0, 1):
            at = pl.ds(half * WIDTH, WIDTH)
            rows = slice(half * depth, (half + 1) * depth)
            keep_ref[other % 4, other // 4, :, at] = keep[rows].astype(LOW)
            send_ref[other % 4, other // 4, :, at] = send[rows].astype(LOW)

    out_back(me_ref, back_ref, gated_ref, out_ref, gated_grad_ref, store)


def shape(*dims, dtype=F32):
    return jax.ShapeDtypeStruct(dims, dtype)


def mixer_scratch(rows):
    return [
        pltpu.VMEM((rows, rows), F32),
        pltpu.VMEM((CONV - 1, rows, LANES), F32),
        pltpu.VMEM((LANES, rows), F32),
        pltpu.VMEM((rows, rows), F32),
    ]


VMEM = pl.BlockSpec(memory_space=pltpu.VMEM)
SMEM = pl.BlockSpec(memory_space=pltpu.SMEM)
ANY = pl.BlockSpec(memory_space=pl.ANY)


def skip_first(kernel, count, *refs):
    kernel(*refs[count:])


def call(kernel, name, flops, size, outs, scratch, *args, awaited=()):
    return pl.pallas_call(
        partial(skip_first, kernel, len(awaited)),
        out_shape=outs,
        in_specs=[ANY] * len(awaited) + [SMEM if item.shape == (1,) else VMEM for item in args],
        out_specs=(VMEM,) * len(outs),
        scratch_shapes=scratch,
        compiler_params=pltpu.CompilerParams(vmem_limit_bytes=VMEM_LIMIT),
        cost_estimate=pl.CostEstimate(flops=flops, bytes_accessed=size, transcendentals=0),
        name=name,
    )(*awaited, *args)


def forward(resid, in_full, small, segs, *awaited):
    rows = resid.shape[0]
    outs = (
        shape(rows, PADDED), shape(rows, INNER), shape(rows, WIDTH, dtype=LOW), shape(rows, INNER, dtype=LOW),
    )
    scratch = mixer_scratch(rows) + [pltpu.VMEM((rows, INNER), F32)]
    return call(
        forward_kernel, "mix_forward", 10_000_000_000, 10_000_000, outs, scratch,
        resid, in_full, *small, *segs, awaited=awaited,
    )


def backward_out(me, grad, gated, out_full):
    part = shape(4, 4, INNER // PARTS, WIDTH, dtype=LOW)
    outs = (shape(grad.shape[0], INNER), part, part)
    return call(backward_out_kernel, "out_backward", 2_000_000_000, 8_000_000, outs, [], me, grad, gated, out_full)


def backward_mixer(gated_grad, hidden, mixed, small, segs, *awaited):
    rows = hidden.shape[0]
    outs = (shape(rows, PADDED, dtype=LOW), shape(SMALL_ROWS, CONVCH))
    scratch = mixer_scratch(rows) + [
        pltpu.VMEM((rows, rows), F32), pltpu.VMEM((rows, CONVCH), F32), pltpu.VMEM((rows, CONVCH), F32),
    ]
    return call(
        backward_mixer_kernel, "mix_backward", 12_000_000_000, 5_000_000, outs, scratch,
        gated_grad, hidden, mixed, *small[1:], *segs, awaited=awaited,
    )


def backward_in(me, grad, resid, normed, dhidden, in_full, norm, *awaited):
    rows = resid.shape[0]
    part = shape(4, 4, WIDTH // PARTS, PADDED, dtype=LOW)
    outs = (shape(rows, WIDTH), part, part)
    scratch = [
        pltpu.VMEM((WIDTH, 3 * LANES), F32), pltpu.VMEM((WIDTH, rows), LOW), pltpu.VMEM((rows, WIDTH), F32),
    ]
    return call(
        backward_in_kernel, "in_backward", 6_000_000_000, 14_000_000, outs, scratch,
        me, grad, resid, normed, dhidden, in_full, norm, awaited=awaited,
    )


def backward_both(me, grad, resid, normed, dhidden, in_full, norm, gated, out_full, *awaited):
    rows = resid.shape[0]
    part = shape(4, 4, WIDTH // PARTS, 2 * WIDTH + PADDED, dtype=LOW)
    outs = (shape(rows, WIDTH), part, part, shape(rows, INNER))
    scratch = [
        pltpu.VMEM((WIDTH, 3 * LANES), F32), pltpu.VMEM((WIDTH, rows), LOW), pltpu.VMEM((rows, WIDTH), F32),
    ]
    return call(
        backward_both_kernel, "both_backward", 8_000_000_000, 22_000_000, outs, scratch,
        me, grad, resid, normed, dhidden, in_full, norm, gated, out_full, awaited=awaited,
    )


def swap(values, bit, count):
    return lax.ppermute(values, "fsdp", [(index, index ^ bit) for index in range(count)])


def place_kernel(cuts, me_ref, *refs):
    me = me_ref[0]
    whole_refs = refs[10:]
    for core in (0, 1):
        for group, ref in enumerate(refs[5 * core : 5 * core + 5]):
            for item in range(ref.shape[0]):
                away = 2 * (4 * (item + 2 * (group == 4)) + min(group, 3)) + core
                for starts, whole_ref in zip(cuts, whole_refs):
                    for part, low in enumerate(starts):
                        whole_ref[me ^ away, part] = ref[item, :, low : low + whole_ref.shape[3]]


def phase(earlier, *items):
    held = lax.optimization_barrier(tuple(item[0] for item in items) + tuple(earlier))
    return [swap(value, item[1], PARTS) for value, item in zip(held, items)]


def after(earlier, *values):
    return lax.optimization_barrier(tuple(values) + tuple(earlier))[: len(values)]


def along_z(own):
    return [(own, 8), (own, 16), (own, 24)]


def along_xy(cur):
    return [(cur, 2), (cur, 4)]


def across(right, up):
    return [(right[:2], 4), (up[2:], 2)]


def join(own, others):
    return jnp.concatenate([own, *others], axis=0)


def put_together(me, own, *cuts):
    depth = own[0].shape[1]
    other = [swap(piece, 1, PARTS) for piece in own]
    outs = tuple(shape(PARTS, len(starts), depth, width, dtype=LOW) for starts, width in cuts)
    kernel = partial(place_kernel, [starts for starts, width in cuts])
    wholes = call(kernel, "place", 0, 64 * own[0].size, outs, [], me, *own, *other)
    return [whole.reshape(-1, whole.shape[3]) for whole in wholes]


class Sums:
    def __init__(self, keep):
        self.keep = keep

    def add_core(self, other):
        self.other = other

    def local(self, group, low, high):
        return self.keep[group, low:high].astype(F32) + self.other[group, low:high].astype(F32)

    def across(self):
        return [(self.local(3, 0, 2).astype(LOW), 4), (self.local(3, 2, 4).astype(LOW), 2)]

    def along_xy(self, far_a, far_b):
        none = ((0, 0, 0),) * 2
        right = self.local(1, 0, 4) + lax.pad(far_a.astype(F32), 0.0, ((0, 2, 0), *none))
        up = self.local(2, 0, 4) + lax.pad(far_b.astype(F32), 0.0, ((2, 0, 0), *none))
        return [(right.astype(LOW), 2), (up.astype(LOW), 4)]

    def add_xy(self, right, up):
        self.mine = lambda low, high: (
            self.local(0, low, high) + right[low:high].astype(F32) + up[low:high].astype(F32)
        )

    def along_z(self):
        return [(self.mine(item, item + 1).astype(LOW), 8 * item) for item in (1, 2, 3)]

    def result(self, *parts):
        return sum([item.astype(F32) for item in parts], self.mine(0, 1))[0]

    def far_z(self):
        return [(self.mine(2, 4).astype(LOW), 16)]

    def near_z(self, far):
        self.far = far
        return [((self.mine(1, 2) + far[1:].astype(F32)).astype(LOW), 8)]

    def end(self, near):
        return self.result(self.far[:1], near)


def nothing(values):
    return values[(slice(0, 1),) * values.ndim].reshape(()) * 0


class Total:
    def __init__(self, values):
        self.values = values

    def add(self, bit, awaited=None):
        low = self.values.astype(LOW)
        if awaited is not None:
            low = low + nothing(awaited)
        self.values = low.astype(F32) + swap(low, bit, PARTS).astype(F32)


def grow(values, other, me, bit):
    upper = (me & bit) > 0
    return jnp.where(upper, join(other, [values]), join(values, [other]))


def gather_small(values, me, count):
    bit = 1
    while bit < count:
        values = grow(values, swap(values, bit, count), me, bit)
        bit *= 2
    return values


def sum_small(values, count):
    bit = 1
    while bit < count:
        values = values + swap(values, bit, count)
        bit *= 2
    return values


def unpack_kernel(count, fields, packed_ref, *refs):
    packed = packed_ref[...]
    layers = len(refs) // 3
    for item, row, low, width in (
        (0, 0, 0, fields[0]),
        *((1, tap, fields[0] + tap * fields[1], fields[1]) for tap in range(CONV + 1)),
        (2, 0, fields[0] + (CONV + 1) * fields[1], fields[2]),
    ):
        whole = refs[item].shape[1]
        place = iota((1, whole), 1)
        owner = jnp.floor((place.astype(F32) + 0.5) * (1.0 / width)).astype(jnp.int32)
        source = low + place - owner * width
        pick = jnp.where(iota((packed.shape[1], whole), 0) == source, 1.0, 0.0).astype(LOW)
        picked = jnp.dot(packed, pick, preferred_element_type=F32)
        for layer in range(layers):
            mine = iota((packed.shape[0], whole), 0) == owner * layers + layer
            refs[3 * layer + item][row : row + 1, :] = jnp.sum(jnp.where(mine, picked, 0.0), axis=0, keepdims=True)


def head_arrays(log_decay, skip_gain, step_bias):
    heads = jnp.pad(jnp.stack([log_decay, skip_gain, step_bias], axis=1), ((0, 0), (0, 0), (0, LANES - HEADS)))
    return heads, jnp.repeat(skip_gain, HEADDIM, axis=1)[:, None]


def small_arrays(packed, count, fields, held):
    layers = packed.shape[1]
    outs = (shape(1, WIDTH), shape(CONV + 1, CONVCH), shape(1, INNER)) * layers
    rows = packed.reshape(count * layers, packed.shape[2])
    rows = jnp.pad(rows, ((0, 0), (0, -rows.shape[1] % LANES)))
    wide = call(partial(unpack_kernel, count, fields), "unpack", 0, 200_000, outs, [], rows)
    return [[*wide[3 * layer : 3 * layer + 3], *(item[layer] for item in held)] for layer in range(layers)]


def project(resid, gated, out_full):
    return resid + jnp.dot(gated, out_full, preferred_element_type=F32)


def finish(resid, cotangent, segs):
    valid = (segs[0] >= 0).astype(F32)
    return (resid * valid).astype(LOW), cotangent.astype(F32) * valid


def run_plain(count, me, resid, segs, cotangent, in_shards, out_shards, packed, small_of):
    layers = len(in_shards)
    place = (me * 0).astype(jnp.int32).reshape(1)
    packed = gather_small(packed, me, count)
    small = small_of(packed)

    def whole(shard):
        return lax.all_gather(shard, "fsdp", axis=0, tiled=True)

    def scatter(keep, send):
        both = jnp.stack([jnp.swapaxes(keep, 0, 1), jnp.swapaxes(send, 0, 1)], axis=2)
        both = both.reshape(-1, keep.shape[-1]).astype(F32)
        return lax.psum_scatter(both, "fsdp", scatter_dimension=0, tiled=True)

    in_full = [whole(shard) for shard in in_shards]
    out_full = [whole(shard) for shard in out_shards]
    kept = []
    for layer in range(layers):
        saved = forward(resid, in_full[layer], small[layer], segs)
        kept.append((resid, saved))
        resid = project(resid, saved[3], out_full[layer])
    mixed, grad = finish(resid, cotangent, segs)
    in_grads, out_grads, sums = ([None] * layers for item in range(3))
    for layer in reversed(range(layers)):
        resid, (hidden, ssm, normed, gated) = kept[layer]
        gated_grad, out_keep, out_send = backward_out(place, grad, gated, out_full[layer])
        dhidden, sums[layer] = backward_mixer(gated_grad, hidden, ssm, small[layer], segs)
        grad, in_keep, in_send = backward_in(
            place, grad, resid, normed, dhidden, in_full[layer], small[layer][0]
        )
        out_grads[layer] = scatter(out_keep, out_send)
        in_grads[layer] = scatter(in_keep, in_send)
    sums = sum_small(jnp.stack(sums), count)
    return mixed, grad, in_grads, out_grads, sums


def run_staged(me, resid, segs, cotangent, in_shards, out_shards, packed, small_from):
    place = me.astype(jnp.int32).reshape(1)
    depth = in_shards[0].shape[0]
    size = packed.size
    columns = -(-size // depth)
    spare = jnp.pad(packed.reshape(size), (0, columns * depth - size)).reshape(depth, columns)
    in0 = jnp.concatenate(
        [in_shards[0][:, :PROJ], spare, jnp.zeros((depth, PADDED - PROJ - columns), LOW)], axis=1
    )[None]
    in1 = in_shards[1][None]

    def small_of(full):
        held = full[:, PROJ : PROJ + columns].reshape(PARTS, depth * columns)[:, :size]
        return small_from(held.reshape((PARTS,) + packed.shape[1:]))

    out0, out1 = (shard[None] for shard in out_shards)

    others = [swap(in0, bit, PARTS) for bit in (8, 16, 24)]
    cur_a = join(in0, others)
    rest = jnp.concatenate(
        [out0[:, :depth], out0[:, depth:], in1, out1[:, :depth], out1[:, depth:]], axis=2
    ) + nothing(others[0])
    others = [swap(rest, bit, PARTS) for bit in (8, 16, 24)]
    right_a, up_a = phase([], *along_xy(cur_a))
    arrived = sum([nothing(item) for item in others])
    far_a = phase([], *across(right_a + arrived, up_a + arrived))
    arrived = nothing(far_a[0]) + nothing(far_a[1])
    cur_b = join(rest, [item + arrived for item in others])
    right_b, up_b = phase([], *along_xy(cur_b))
    (in0_full,) = put_together(place, [cur_a, right_a, up_a, *far_a], ((0,), PADDED))
    small = small_of(in0_full)
    arrived = nothing(small[0][0]).astype(LOW)
    near_right, near_up = right_b[:2] + arrived, up_b[2:] + arrived
    kept0 = forward(resid, in0_full, small[0], segs, near_right, near_up)
    arrived = nothing(kept0[3])
    far_b = [swap(near_right, 4, PARTS) + arrived, swap(near_up, 2, PARTS) + arrived]
    pieces = [cur_b, right_b, up_b, *far_b]
    start = 2 * WIDTH + PADDED
    out0_full, in1_full, out1_full = put_together(
        place, pieces, ((0, WIDTH), WIDTH), ((2 * WIDTH,), PADDED), ((start, start + WIDTH), WIDTH)
    )
    resid1 = project(resid, kept0[3], out0_full)
    kept1 = forward(resid1, in1_full, small[1], segs)
    mixed, grad = finish(project(resid1, kept1[3], out1_full), cotangent, segs)

    hidden, ssm, normed, gated = kept1
    gated_grad, keep, send = backward_out(place, grad, gated, out1_full)
    sum_c = Sums(keep)
    core = swap(send, 1, PARTS)
    dhidden, small1 = backward_mixer(gated_grad, hidden, ssm, small[1], segs)
    sum_c.add_core(core)

    to_far_c = sum_c.across()
    far_c = phase([], *to_far_c)
    grad, keep, send, gated_grad = backward_both(
        place, grad, resid1, normed, dhidden, in1_full, small[1][0], kept0[3], out0_full,
        *[item[0] for item in to_far_c],
    )
    sum_b = Sums(keep)

    hidden, ssm, normed, gated = kept0
    core = swap(send, 1, PARTS)
    to_xy_c = sum_c.along_xy(*far_c)
    got = phase([], *to_xy_c)
    dhidden, small0 = backward_mixer(
        gated_grad, hidden, ssm, small[0], segs, *[item[0] for item in to_xy_c]
    )
    sums = Total(jnp.stack([small0, small1]))
    sum_b.add_core(core)
    sum_c.add_xy(*got)

    to_far_b = sum_b.across()
    far_b = phase([], *to_far_b)
    (far_c,) = phase([], *sum_c.far_z())
    sums.add(1)
    grad, keep, send = backward_in(
        place, grad, resid, normed, dhidden, in0_full, small[0][0], *[item[0] for item in to_far_b]
    )
    sum_a = Sums(keep)

    core = swap(send, 1, PARTS)
    to_xy = sum_b.along_xy(*far_b)
    right_b, up_b = phase([], *to_xy)
    (near_c,) = phase([], *sum_c.near_z(far_c))
    sums.add(8)
    sum_a.add_core(core)
    far_a = phase([], *sum_a.across())
    sums.add(16)
    to_xy = sum_a.along_xy(*far_a)
    sum_b.add_xy(right_b, up_b)
    right_a, up_a = phase([], *to_xy)
    (far_b,) = phase([], (sum_b.far_z()[0][0], 16))
    sum_a.add_xy(right_a, up_a)
    to_z = sum_a.along_z()
    parts = phase([], *to_z)
    sums.add(2, to_z[0][0])
    sums.add(4)
    (near_b,) = phase([], *sum_b.near_z(far_b))
    both = sum_b.end(near_b)
    in_grads = [sum_a.result(*parts), both[:, 2 * WIDTH :]]
    out_grads = [jnp.concatenate([both[:, :WIDTH], both[:, WIDTH : 2 * WIDTH]]), sum_c.end(near_c)]
    return mixed, grad, in_grads, out_grads, sums.values


def body(
    count, tokens, segments, norm_gain, in_weight, conv_weight, conv_bias,
    log_decay, skip_gain, step_bias, gate_gain, out_weight, cotangent,
):
    layers, in_rows = in_weight.shape[:2]
    rows = tokens.shape[0] * BLOCK
    me = lax.axis_index("fsdp")
    chans, gates = conv_bias.shape[1], gate_gain.shape[1]
    packed = jnp.concatenate([norm_gain, conv_weight.reshape(layers, -1), conv_bias, gate_gain], axis=1)[None]
    padded = jnp.pad(in_weight, ((0, 0), (0, 0), (0, PADDED - PROJ)))
    segs = (segments.reshape(rows, 1), segments.reshape(1, rows))

    held = head_arrays(log_decay, skip_gain, step_bias)

    def small_of(packed):
        return small_arrays(packed, count, (in_rows, chans, gates), held)

    run = run_staged if count == PARTS and layers == 2 else partial(run_plain, count)
    mixed, grad, in_grads, out_grads, sums = run(
        me, tokens.reshape(rows, WIDTH).astype(F32), segs, cotangent.reshape(rows, WIDTH),
        [padded[layer] for layer in range(layers)], [out_weight[layer] for layer in range(layers)], packed, small_of,
    )
    total = sums

    def own(values, size):
        return lax.dynamic_slice_in_dim(values, me * size, size, axis=values.ndim - 1)

    by_head = total[:, 7, :INNER].reshape(layers, HEADS, HEADDIM).sum(axis=-1)
    return (
        mixed.reshape(tokens.shape),
        grad.reshape(tokens.shape),
        jnp.stack([item[:, PROJ] for item in in_grads]),
        jnp.stack([item[:, :PROJ] for item in in_grads]),
        own(total[:, 1 : 1 + CONV], chans),
        own(total[:, 5], chans),
        total[:, 0, :HEADS],
        by_head,
        total[:, 0, LANES : LANES + HEADS],
        own(total[:, 6, :INNER], gates),
        jnp.stack(out_grads),
    )


def solution(mesh):
    split0 = P("fsdp", None, None)
    split1 = P(None, "fsdp", None)
    in_specs = (
        split0, P("fsdp", None), P(None, "fsdp"), split1, P(None, None, "fsdp"), P(None, "fsdp"),
        P(), P(), P(), P(None, "fsdp"), split1, split0,
    )
    out_specs = (
        split0, split0, P(None, "fsdp"), split1, P(None, None, "fsdp"), P(None, "fsdp"),
        P(), P(), P(), P(None, "fsdp"), split1,
    )
    return jax.shard_map(
        partial(body, mesh.shape["fsdp"]), mesh=mesh, in_specs=in_specs, out_specs=out_specs, check_vma=False
    )
```

```python
from functools import partial

import jax
import jax.numpy as jnp
from jax import lax
from jax.experimental import pallas as pl
from jax.experimental.pallas import tpu as pltpu
from jax.sharding import PartitionSpec as P

HEADS = 24
HEADDIM = 64
STATE = 128
CONV = 4
BLOCK = 64
WIDTH = 768
INNER = HEADS * HEADDIM
CONVCH = INNER + 2 * STATE
PROJ = INNER + CONVCH + HEADS
LANES = 128
PADDED = INNER + CONVCH + LANES
PAIRS = INNER // LANES
STEP_AT = INNER + CONVCH
SMALL_ROWS = 8
PARTS = 32
EPSILON = 1e-05
EXACT = lax.Precision.HIGHEST
F32 = jnp.float32
LOW = jnp.bfloat16
NT = (((1,), (1,)), ((), ()))
TN = (((0,), (0,)), ((), ()))
VMEM_LIMIT = 56 * 1024 * 1024


def tile(index):
    return pl.ds(pl.multiple_of(index * LANES, LANES), LANES)


def iota(shape, dim):
    return lax.broadcasted_iota(jnp.int32, shape, dim)


def split(values):
    high = values.astype(LOW)
    return high, (values - high.astype(F32)).astype(LOW)


def low_half():
    return iota((1, LANES), 1) < HEADDIM


def set_masks(seg_col, seg_row, allowed_ref, taps_ref):
    rows = seg_col.shape[0]
    t, s = iota((rows, rows), 0), iota((rows, rows), 1)
    tri = (t >= s) & (t // BLOCK == s // BLOCK)
    allowed_ref[...] = jnp.where(tri & (seg_col == seg_row), 1.0, 0.0)
    wide = jnp.broadcast_to(seg_col, (rows, LANES))
    place = iota((rows, LANES), 0) % BLOCK
    for tap in range(1, CONV):
        earlier = pltpu.roll(wide, tap, axis=0)
        taps_ref[tap - 1] = jnp.where((earlier == wide) & (place >= tap), 1.0, 0.0)
    return jnp.where(tri, 1.0, 0.0)


def conv_tile(signal, weight_ref, taps_ref, at):
    total = weight_ref[CONV : CONV + 1, at] + signal * weight_ref[CONV - 1 : CONV, at]
    for tap in range(1, CONV):
        shifted = pltpu.roll(signal, tap, axis=0) * taps_ref[tap - 1]
        total = total + shifted * weight_ref[CONV - 1 - tap : CONV - tap, at]
    return total


def steps(raw, heads_ref):
    raw = raw + heads_ref[2:3]
    step = jnp.maximum(raw, 0.0) + jnp.log1p(jnp.exp(-jnp.abs(raw)))
    return raw, step, step * -jnp.exp(heads_ref[0:1])


def spread_heads(high, low, index):
    head = iota((LANES, LANES), 0)
    lane = iota((LANES, LANES), 1)
    pick = jnp.where(head == 2 * index + lane // HEADDIM, 1.0, 0.0).astype(LOW)
    return jnp.dot(high, pick, preferred_element_type=F32) + jnp.dot(
        low, pick, preferred_element_type=F32
    )


def decays(turned_ref, allowed, head):
    rows = allowed.shape[0]
    across = jnp.broadcast_to(turned_ref[pl.ds(head, 1), :], (rows, rows))
    gaps = jnp.where(allowed > 0.0, across.T - across, -1e30)
    return jnp.exp(gaps)


def forward_kernel(
    resid_ref, in_ref, norm_ref, conv_ref, gate_ref, heads_ref, skip_ref, col_ref, row_ref,
    hidden_ref, mixed_ref, normed_ref, gated_ref,
    allowed_ref, taps_ref, turned_ref, scores_ref, product_ref,
):
    tri = set_masks(col_ref[...], row_ref[...], allowed_ref, taps_ref)
    resid = resid_ref[...]
    scale = lax.rsqrt(jnp.mean(resid * resid, axis=-1, keepdims=True) + EPSILON)
    normed_ref[...] = (resid * scale * norm_ref[...]).astype(LOW)

    def project(index, carry):
        at = pl.ds(pl.multiple_of(index * 3 * LANES, LANES), 3 * LANES)
        hidden_ref[:, at] = jnp.dot(normed_ref[...], in_ref[:, at], preferred_element_type=F32)
        return carry

    lax.fori_loop(0, PADDED // (3 * LANES), project, 0)
    raw, step, rate = steps(hidden_ref[:, STEP_AT:], heads_ref)
    turned_ref[...] = jnp.dot(tri, rate, precision=EXACT, preferred_element_type=F32).T
    high, low = split(step)
    pair = []
    for index in (0, 1):
        at = pl.ds(INNER + index * STATE, STATE)
        total = conv_tile(hidden_ref[:, pl.ds(2 * INNER + index * STATE, STATE)], conv_ref, taps_ref, at)
        pair.append(total * jax.nn.sigmoid(total))
    scores_ref[...] = lax.dot_general(pair[1], pair[0], NT, precision=EXACT, preferred_element_type=F32)
    first = low_half()

    def heads(index, squares):
        at = tile(index)
        total = conv_tile(hidden_ref[:, tile(index + PAIRS)], conv_ref, taps_ref, at)
        values = total * jax.nn.sigmoid(total)
        scaled = values * spread_heads(high, low, index)
        allowed = allowed_ref[...]
        scores = scores_ref[...]
        weights = jnp.concatenate(
            [(scores * decays(turned_ref, allowed, 2 * index + head)).astype(LOW) for head in (0, 1)], axis=1
        )
        both = jnp.concatenate([jnp.where(first, scaled, 0.0), jnp.where(first, 0.0, scaled)], axis=0).astype(LOW)
        mixed = jnp.dot(weights, both, preferred_element_type=F32)
        mixed_ref[:, at] = mixed
        gate = hidden_ref[:, at]
        product = (mixed + values * skip_ref[:, at]) * (gate * jax.nn.sigmoid(gate))
        product_ref[:, at] = product
        return squares + product * product

    squares = lax.fori_loop(0, PAIRS, heads, jnp.zeros((resid.shape[0], LANES), F32))
    scale = lax.rsqrt(jnp.sum(squares, axis=-1, keepdims=True) / INNER + EPSILON)
    gated_ref[...] = (product_ref[...] * scale * gate_ref[...]).astype(LOW)


def out_back(me_ref, grad_ref, gated_ref, out_ref, gated_grad_ref, store):
    core = me_ref[0] % 2
    chip = me_ref[0] // 2
    grad_low = grad_ref[...].astype(LOW)
    depth = INNER // PARTS
    pairs = 3 * LANES // (2 * depth)

    def step(index, carry):
        at = pl.ds(pl.multiple_of(index * 3 * LANES, LANES), 3 * LANES)
        gated_grad_ref[:, at] = lax.dot_general(grad_low, out_ref[at, :], NT, preferred_element_type=F32)
        part = lax.dot_general(gated_ref[:, at], grad_low, TN, preferred_element_type=F32)
        for pair in range(pairs):
            even = part[2 * pair * depth : (2 * pair + 1) * depth]
            odd = part[(2 * pair + 1) * depth : (2 * pair + 2) * depth]
            store((index * pairs + pair) ^ chip, jnp.where(core == 0, even, odd), jnp.where(core == 0, odd, even))
        return carry

    lax.fori_loop(0, INNER // (3 * LANES), step, 0)


def backward_out_kernel(me_ref, grad_ref, gated_ref, out_ref, gated_grad_ref, keep_ref, send_ref):
    def store(other, keep, send):
        keep_ref[other % 4, other // 4] = keep.astype(LOW)
        send_ref[other % 4, other // 4] = send.astype(LOW)

    out_back(me_ref, grad_ref, gated_ref, out_ref, gated_grad_ref, store)


def backward_mixer_kernel(
    gated_grad_ref, hidden_ref, mixed_ref, conv_ref, gate_ref, heads_ref, skip_ref, col_ref, row_ref,
    dhidden_ref, small_ref,
    allowed_ref, taps_ref, turned_ref, scores_ref, dscores_ref, values_ref, slope_ref,
):
    tri = set_masks(col_ref[...], row_ref[...], allowed_ref, taps_ref)
    rows = hidden_ref.shape[0]
    small_ref[...] = jnp.zeros_like(small_ref)
    raw, step, rate = steps(hidden_ref[:, STEP_AT:], heads_ref)
    turned_ref[...] = jnp.dot(tri, rate, precision=EXACT, preferred_element_type=F32).T
    high, low = split(step)

    def again(index, carry):
        at = tile(index)
        total = conv_tile(hidden_ref[:, tile(index + PAIRS)], conv_ref, taps_ref, at)
        sigmoid = jax.nn.sigmoid(total)
        values_ref[:, at] = total * sigmoid
        slope_ref[:, at] = sigmoid * (1.0 + total * (1.0 - sigmoid))
        return carry

    lax.fori_loop(0, PAIRS + 2, again, 0)
    inputs_b = values_ref[:, INNER : INNER + STATE]
    outputs_c = values_ref[:, INNER + STATE :]
    scores_ref[...] = lax.dot_general(outputs_c, inputs_b, NT, precision=EXACT, preferred_element_type=F32)
    dscores_ref[...] = jnp.zeros_like(dscores_ref)

    def measure(index, carry):
        squares, dots = carry
        at = tile(index)
        gate = hidden_ref[:, at]
        product = (mixed_ref[:, at] + values_ref[:, at] * skip_ref[:, at]) * (gate * jax.nn.sigmoid(gate))
        return squares + product * product, dots + product * gated_grad_ref[:, at] * gate_ref[:, at]

    zero = jnp.zeros((rows, LANES), F32)
    squares, dots = lax.fori_loop(0, PAIRS, measure, (zero, zero))
    scale = lax.rsqrt(jnp.sum(squares, axis=-1, keepdims=True) / INNER + EPSILON)
    pull = scale * scale * scale * (jnp.sum(dots, axis=-1, keepdims=True) / INNER)
    first = low_half()

    def conv_back(index, du):
        at = tile(index)
        signal = hidden_ref[:, tile(index + PAIRS)]
        small_ref[5:6, at] = jnp.sum(du, axis=0, keepdims=True)
        small_ref[CONV : CONV + 1, at] = jnp.sum(du * signal, axis=0, keepdims=True)
        total = du * conv_ref[CONV - 1 : CONV, at]
        for tap in range(1, CONV):
            masked = du * taps_ref[tap - 1]
            shifted = pltpu.roll(signal, tap, axis=0)
            small_ref[CONV - tap : CONV - tap + 1, at] = jnp.sum(masked * shifted, axis=0, keepdims=True)
            total = total + pltpu.roll(masked, rows - tap, axis=0) * conv_ref[CONV - 1 - tap : CONV - tap, at]
        dhidden_ref[:, tile(index + PAIRS)] = total.astype(LOW)

    def heads(index, carry):
        dcum, dstep = carry
        at = tile(index)
        gate = hidden_ref[:, at]
        sigmoid = jax.nn.sigmoid(gate)
        silu = gate * sigmoid
        values = values_ref[:, at]
        mixed = mixed_ref[:, at]
        skip = skip_ref[:, at]
        states = mixed + values * skip
        product = states * silu
        gated_grad = gated_grad_ref[:, at]
        small_ref[6:7, at] = jnp.sum(gated_grad * product * scale, axis=0, keepdims=True)
        dproduct = scale * (gated_grad * gate_ref[:, at]) - product * pull
        dhidden_ref[:, at] = (dproduct * states * (sigmoid * (1.0 + gate * (1.0 - sigmoid)))).astype(LOW)
        dstates = dproduct * silu
        small_ref[7:8, at] = jnp.sum(dstates * values, axis=0, keepdims=True)
        step_wide = spread_heads(high, low, index)
        scaled = (values * step_wide).astype(LOW)
        dlow = dstates.astype(LOW)
        none = jnp.zeros_like(dlow)
        stacked = jnp.concatenate([jnp.where(first, dlow, none), jnp.where(first, none, dlow)], axis=0)
        allowed = allowed_ref[...]
        scores = scores_ref[...]
        factors = [decays(turned_ref, allowed, 2 * index + head) for head in (0, 1)]
        weights = jnp.concatenate([(scores * factor).astype(LOW) for factor in factors], axis=0)
        dweights = lax.dot_general(stacked, scaled, NT, preferred_element_type=F32)
        dscores_ref[...] += dweights[:rows] * factors[0] + dweights[rows:] * factors[1]
        dscaled = lax.dot_general(weights, stacked, TN, preferred_element_type=F32)
        head = iota((LANES, LANES), 1)
        lane = iota((LANES, LANES), 0)
        pick = jnp.where(head == 2 * index + lane // HEADDIM, 1.0, 0.0).astype(LOW)
        gained = split(dlow.astype(F32) * mixed - scaled.astype(F32) * dscaled)
        dcum = dcum + sum(jnp.dot(item, pick, preferred_element_type=F32) for item in gained)
        gained = split(values * dscaled)
        dstep = dstep + sum(jnp.dot(item, pick, preferred_element_type=F32) for item in gained)
        dvalues = step_wide * dscaled + skip * dstates
        conv_back(index, dvalues * slope_ref[:, at])
        return dcum, dstep

    dcum, dstep = lax.fori_loop(0, PAIRS, heads, (zero, zero))
    dscores = dscores_ref[...]
    dinputs = lax.dot_general(dscores, outputs_c, TN, precision=EXACT, preferred_element_type=F32)
    doutputs = jnp.dot(dscores, inputs_b, precision=EXACT, preferred_element_type=F32)
    conv_back(PAIRS, dinputs * slope_ref[:, INNER : INNER + STATE])
    conv_back(PAIRS + 1, doutputs * slope_ref[:, INNER + STATE :])
    drate = lax.dot_general(tri, dcum, TN, precision=EXACT, preferred_element_type=F32)
    small_ref[0:1, :LANES] = jnp.sum(drate * rate, axis=0, keepdims=True)
    draw = (dstep - drate * jnp.exp(heads_ref[0:1])) * jax.nn.sigmoid(raw)
    small_ref[0:1, LANES : 2 * LANES] = jnp.sum(draw, axis=0, keepdims=True)
    dhidden_ref[:, STEP_AT:] = draw.astype(LOW)


def backward_in_kernel(
    me_ref, grad_ref, resid_ref, normed_ref, dhidden_ref, in_ref, norm_ref,
    back_ref, in_keep_ref, in_send_ref,
    gathered_ref, turned_norm_ref, dnorm_ref, first=0,
):
    core = me_ref[0] % 2
    chip = me_ref[0] // 2
    turned_norm_ref[...] = normed_ref[...].T
    dnorm_ref[...] = jnp.zeros_like(dnorm_ref)

    def in_back(index, carry):
        at = pl.ds(pl.multiple_of(index * 3 * LANES, LANES), 3 * LANES)
        to = pl.ds(pl.multiple_of(first + index * 3 * LANES, LANES), 3 * LANES)
        dhidden = dhidden_ref[:, at]
        dnorm_ref[...] += lax.dot_general(dhidden, in_ref[:, at], NT, preferred_element_type=F32)
        gathered_ref[...] = jnp.dot(turned_norm_ref[...], dhidden, preferred_element_type=F32)
        store(slice(None), to)
        return carry

    def store(part, to):
        depth = WIDTH // PARTS
        for pair in range(PARTS // 2):
            even = gathered_ref[2 * pair * depth : (2 * pair + 1) * depth, part]
            odd = gathered_ref[(2 * pair + 1) * depth : (2 * pair + 2) * depth, part]
            other = pair ^ chip
            in_keep_ref[other % 4, other // 4, :, to] = jnp.where(core == 0, even, odd).astype(LOW)
            in_send_ref[other % 4, other // 4, :, to] = jnp.where(core == 0, odd, even).astype(LOW)

    lax.fori_loop(0, PADDED // (3 * LANES), in_back, 0)
    resid = resid_ref[...]
    scale = lax.rsqrt(jnp.mean(resid * resid, axis=-1, keepdims=True) + EPSILON)
    dnorm = dnorm_ref[...]
    norm_grad = jnp.sum(dnorm * resid * scale, axis=0, keepdims=True)
    column = jnp.broadcast_to(norm_grad, (LANES, WIDTH)).T
    spare = iota((1, LANES), 1) == HEADS
    gathered_ref[:, 2 * LANES :] = jnp.where(spare, column, gathered_ref[:, 2 * LANES :])
    store(slice(2 * LANES, 3 * LANES), pl.ds(first + STEP_AT, LANES))
    gained = dnorm * norm_ref[...]
    pull = scale * scale * scale * jnp.mean(gained * resid, axis=-1, keepdims=True)
    back_ref[...] = grad_ref[...] + scale * gained - resid * pull


def backward_both_kernel(
    me_ref, grad_ref, resid_ref, normed_ref, dhidden_ref, in_ref, norm_ref, gated_ref, out_ref,
    back_ref, keep_ref, send_ref, gated_grad_ref, *scratch,
):
    backward_in_kernel(
        me_ref, grad_ref, resid_ref, normed_ref, dhidden_ref, in_ref, norm_ref,
        back_ref, keep_ref, send_ref, *scratch, first=2 * WIDTH,
    )
    depth = WIDTH // PARTS

    def store(other, keep, send):
        for half in (0, 1):
            at = pl.ds(half * WIDTH, WIDTH)
            rows = slice(half * depth, (half + 1) * depth)
            keep_ref[other % 4, other // 4, :, at] = keep[rows].astype(LOW)
            send_ref[other % 4, other // 4, :, at] = send[rows].astype(LOW)

    out_back(me_ref, back_ref, gated_ref, out_ref, gated_grad_ref, store)


def shape(*dims, dtype=F32):
    return jax.ShapeDtypeStruct(dims, dtype)


def mixer_scratch(rows):
    return [
        pltpu.VMEM((rows, rows), F32),
        pltpu.VMEM((CONV - 1, rows, LANES), F32),
        pltpu.VMEM((LANES, rows), F32),
        pltpu.VMEM((rows, rows), F32),
    ]


VMEM = pl.BlockSpec(memory_space=pltpu.VMEM)
SMEM = pl.BlockSpec(memory_space=pltpu.SMEM)
ANY = pl.BlockSpec(memory_space=pl.ANY)


def skip_first(kernel, count, *refs):
    kernel(*refs[count:])


def call(kernel, name, flops, size, outs, scratch, *args, awaited=()):
    return pl.pallas_call(
        partial(skip_first, kernel, len(awaited)),
        out_shape=outs,
        in_specs=[ANY] * len(awaited) + [SMEM if item.shape == (1,) else VMEM for item in args],
        out_specs=(VMEM,) * len(outs),
        scratch_shapes=scratch,
        compiler_params=pltpu.CompilerParams(vmem_limit_bytes=VMEM_LIMIT),
        cost_estimate=pl.CostEstimate(flops=flops, bytes_accessed=size, transcendentals=0),
        name=name,
    )(*awaited, *args)


def forward(resid, in_full, small, segs, *awaited):
    rows = resid.shape[0]
    outs = (
        shape(rows, PADDED), shape(rows, INNER), shape(rows, WIDTH, dtype=LOW), shape(rows, INNER, dtype=LOW),
    )
    scratch = mixer_scratch(rows) + [pltpu.VMEM((rows, INNER), F32)]
    return call(
        forward_kernel, "mix_forward", 10_000_000_000, 10_000_000, outs, scratch,
        resid, in_full, *small, *segs, awaited=awaited,
    )


def backward_out(me, grad, gated, out_full):
    part = shape(4, 4, INNER // PARTS, WIDTH, dtype=LOW)
    outs = (shape(grad.shape[0], INNER), part, part)
    return call(backward_out_kernel, "out_backward", 2_000_000_000, 8_000_000, outs, [], me, grad, gated, out_full)


def backward_mixer(gated_grad, hidden, mixed, small, segs, *awaited):
    rows = hidden.shape[0]
    outs = (shape(rows, PADDED, dtype=LOW), shape(SMALL_ROWS, CONVCH))
    scratch = mixer_scratch(rows) + [
        pltpu.VMEM((rows, rows), F32), pltpu.VMEM((rows, CONVCH), F32), pltpu.VMEM((rows, CONVCH), F32),
    ]
    return call(
        backward_mixer_kernel, "mix_backward", 12_000_000_000, 5_000_000, outs, scratch,
        gated_grad, hidden, mixed, *small[1:], *segs, awaited=awaited,
    )


def backward_in(me, grad, resid, normed, dhidden, in_full, norm, *awaited):
    rows = resid.shape[0]
    part = shape(4, 4, WIDTH // PARTS, PADDED, dtype=LOW)
    outs = (shape(rows, WIDTH), part, part)
    scratch = [
        pltpu.VMEM((WIDTH, 3 * LANES), F32), pltpu.VMEM((WIDTH, rows), LOW), pltpu.VMEM((rows, WIDTH), F32),
    ]
    return call(
        backward_in_kernel, "in_backward", 6_000_000_000, 14_000_000, outs, scratch,
        me, grad, resid, normed, dhidden, in_full, norm, awaited=awaited,
    )


def backward_both(me, grad, resid, normed, dhidden, in_full, norm, gated, out_full, *awaited):
    rows = resid.shape[0]
    part = shape(4, 4, WIDTH // PARTS, 2 * WIDTH + PADDED, dtype=LOW)
    outs = (shape(rows, WIDTH), part, part, shape(rows, INNER))
    scratch = [
        pltpu.VMEM((WIDTH, 3 * LANES), F32), pltpu.VMEM((WIDTH, rows), LOW), pltpu.VMEM((rows, WIDTH), F32),
    ]
    return call(
        backward_both_kernel, "both_backward", 8_000_000_000, 22_000_000, outs, scratch,
        me, grad, resid, normed, dhidden, in_full, norm, gated, out_full, awaited=awaited,
    )


def swap(values, bit, count):
    return lax.ppermute(values, "fsdp", [(index, index ^ bit) for index in range(count)])


def place_kernel(cuts, me_ref, *refs):
    me = me_ref[0]
    whole_refs = refs[10:]
    for core in (0, 1):
        for group, ref in enumerate(refs[5 * core : 5 * core + 5]):
            for item in range(ref.shape[0]):
                away = 2 * (4 * (item + 2 * (group == 4)) + min(group, 3)) + core
                for starts, whole_ref in zip(cuts, whole_refs):
                    for part, low in enumerate(starts):
                        whole_ref[me ^ away, part] = ref[item, :, low : low + whole_ref.shape[3]]


def phase(earlier, *items):
    held = lax.optimization_barrier(tuple(item[0] for item in items) + tuple(earlier))
    return [swap(value, item[1], PARTS) for value, item in zip(held, items)]


def after(earlier, *values):
    return lax.optimization_barrier(tuple(values) + tuple(earlier))[: len(values)]


def along_z(own):
    return [(own, 8), (own, 16), (own, 24)]


def along_xy(cur):
    return [(cur, 2), (cur, 4)]


def across(right, up):
    return [(right[:2], 4), (up[2:], 2)]


def join(own, others):
    return jnp.concatenate([own, *others], axis=0)


def put_together(me, own, *cuts):
    depth = own[0].shape[1]
    other = [swap(piece, 1, PARTS) for piece in own]
    outs = tuple(shape(PARTS, len(starts), depth, width, dtype=LOW) for starts, width in cuts)
    kernel = partial(place_kernel, [starts for starts, width in cuts])
    wholes = call(kernel, "place", 0, 64 * own[0].size, outs, [], me, *own, *other)
    return [whole.reshape(-1, whole.shape[3]) for whole in wholes]


class Sums:
    def __init__(self, keep):
        self.keep = keep

    def add_core(self, other):
        self.other = other

    def local(self, group, low, high):
        return self.keep[group, low:high].astype(F32) + self.other[group, low:high].astype(F32)

    def across(self):
        return [(self.local(3, 0, 2).astype(LOW), 4), (self.local(3, 2, 4).astype(LOW), 2)]

    def along_xy(self, far_a, far_b):
        none = ((0, 0, 0),) * 2
        right = self.local(1, 0, 4) + lax.pad(far_a.astype(F32), 0.0, ((0, 2, 0), *none))
        up = self.local(2, 0, 4) + lax.pad(far_b.astype(F32), 0.0, ((2, 0, 0), *none))
        return [(right.astype(LOW), 2), (up.astype(LOW), 4)]

    def add_xy(self, right, up):
        self.mine = lambda low, high: (
            self.local(0, low, high) + right[low:high].astype(F32) + up[low:high].astype(F32)
        )

    def along_z(self):
        return [(self.mine(item, item + 1).astype(LOW), 8 * item) for item in (1, 2, 3)]

    def result(self, *parts):
        return sum([item.astype(F32) for item in parts], self.mine(0, 1))[0]

    def far_z(self):
        return [(self.mine(2, 4).astype(LOW), 16)]

    def near_z(self, far):
        self.far = far
        return [((self.mine(1, 2) + far[1:].astype(F32)).astype(LOW), 8)]

    def end(self, near):
        return self.result(self.far[:1], near)


def nothing(values):
    return values[(slice(0, 1),) * values.ndim].reshape(()) * 0


class Total:
    def __init__(self, first, second, me):
        self.even = me % 2 == 0
        self.values = jnp.where(self.even, first, second)
        self.values += swap(jnp.where(self.even, second, first), 1, PARTS)

    def add(self, bit, awaited=None):
        values = self.values
        if awaited is not None:
            values = values + nothing(awaited).astype(F32)
        self.values = values + swap(values, bit, PARTS)

    def both(self):
        other = swap(self.values, 1, PARTS)
        return jnp.stack([jnp.where(self.even, self.values, other), jnp.where(self.even, other, self.values)])


def grow(values, other, me, bit):
    upper = (me & bit) > 0
    return jnp.where(upper, join(other, [values]), join(values, [other]))


def gather_small(values, me, count):
    bit = 1
    while bit < count:
        values = grow(values, swap(values, bit, count), me, bit)
        bit *= 2
    return values


def sum_small(values, count):
    bit = 1
    while bit < count:
        values = values + swap(values, bit, count)
        bit *= 2
    return values


def unpack_kernel(count, fields, packed_ref, *refs):
    packed = packed_ref[...]
    layers = len(refs) // 3
    for item, row, low, width in (
        (0, 0, 0, fields[0]),
        *((1, tap, fields[0] + tap * fields[1], fields[1]) for tap in range(CONV + 1)),
        (2, 0, fields[0] + (CONV + 1) * fields[1], fields[2]),
    ):
        whole = refs[item].shape[1]
        place = iota((1, whole), 1)
        owner = jnp.floor((place.astype(F32) + 0.5) * (1.0 / width)).astype(jnp.int32)
        source = low + place - owner * width
        pick = jnp.where(iota((packed.shape[1], whole), 0) == source, 1.0, 0.0).astype(LOW)
        picked = jnp.dot(packed, pick, preferred_element_type=F32)
        for layer in range(layers):
            mine = iota((packed.shape[0], whole), 0) == owner * layers + layer
            refs[3 * layer + item][row : row + 1, :] = jnp.sum(jnp.where(mine, picked, 0.0), axis=0, keepdims=True)


def head_arrays(log_decay, skip_gain, step_bias):
    heads = jnp.pad(jnp.stack([log_decay, skip_gain, step_bias], axis=1), ((0, 0), (0, 0), (0, LANES - HEADS)))
    return heads, jnp.repeat(skip_gain, HEADDIM, axis=1)[:, None]


def small_arrays(packed, count, fields, held):
    layers = packed.shape[1]
    outs = (shape(1, WIDTH), shape(CONV + 1, CONVCH), shape(1, INNER)) * layers
    rows = packed.reshape(count * layers, packed.shape[2])
    rows = jnp.pad(rows, ((0, 0), (0, -rows.shape[1] % LANES)))
    wide = call(partial(unpack_kernel, count, fields), "unpack", 0, 200_000, outs, [], rows)
    return [[*wide[3 * layer : 3 * layer + 3], *(item[layer] for item in held)] for layer in range(layers)]


def project(resid, gated, out_full):
    return resid + jnp.dot(gated, out_full, preferred_element_type=F32)


def finish(resid, cotangent, segs):
    valid = (segs[0] >= 0).astype(F32)
    return (resid * valid).astype(LOW), cotangent.astype(F32) * valid


def run_plain(count, me, resid, segs, cotangent, in_shards, out_shards, packed, small_of):
    layers = len(in_shards)
    place = (me * 0).astype(jnp.int32).reshape(1)
    packed = gather_small(packed, me, count)
    small = small_of(packed)

    def whole(shard):
        return lax.all_gather(shard, "fsdp", axis=0, tiled=True)

    def scatter(keep, send):
        both = jnp.stack([jnp.swapaxes(keep, 0, 1), jnp.swapaxes(send, 0, 1)], axis=2)
        both = both.reshape(-1, keep.shape[-1]).astype(F32)
        return lax.psum_scatter(both, "fsdp", scatter_dimension=0, tiled=True)

    in_full = [whole(shard) for shard in in_shards]
    out_full = [whole(shard) for shard in out_shards]
    kept = []
    for layer in range(layers):
        saved = forward(resid, in_full[layer], small[layer], segs)
        kept.append((resid, saved))
        resid = project(resid, saved[3], out_full[layer])
    mixed, grad = finish(resid, cotangent, segs)
    in_grads, out_grads, sums = ([None] * layers for item in range(3))
    for layer in reversed(range(layers)):
        resid, (hidden, ssm, normed, gated) = kept[layer]
        gated_grad, out_keep, out_send = backward_out(place, grad, gated, out_full[layer])
        dhidden, sums[layer] = backward_mixer(gated_grad, hidden, ssm, small[layer], segs)
        grad, in_keep, in_send = backward_in(
            place, grad, resid, normed, dhidden, in_full[layer], small[layer][0]
        )
        out_grads[layer] = scatter(out_keep, out_send)
        in_grads[layer] = scatter(in_keep, in_send)
    sums = sum_small(jnp.stack(sums), count)
    return mixed, grad, in_grads, out_grads, sums


def run_staged(me, resid, segs, cotangent, in_shards, out_shards, packed, small_from):
    place = me.astype(jnp.int32).reshape(1)
    depth = in_shards[0].shape[0]
    size = packed.size
    columns = -(-size // depth)
    spare = jnp.pad(packed.reshape(size), (0, columns * depth - size)).reshape(depth, columns)
    in0 = jnp.concatenate(
        [in_shards[0][:, :PROJ], spare, jnp.zeros((depth, PADDED - PROJ - columns), LOW)], axis=1
    )[None]
    in1 = in_shards[1][None]

    def small_of(full):
        held = full[:, PROJ : PROJ + columns].reshape(PARTS, depth * columns)[:, :size]
        return small_from(held.reshape((PARTS,) + packed.shape[1:]))

    out0, out1 = (shard[None] for shard in out_shards)

    others = [swap(in0, bit, PARTS) for bit in (8, 16, 24)]
    cur_a = join(in0, others)
    rest = jnp.concatenate(
        [out0[:, :depth], out0[:, depth:], in1, out1[:, :depth], out1[:, depth:]], axis=2
    ) + nothing(others[0])
    others = [swap(rest, bit, PARTS) for bit in (8, 16, 24)]
    right_a, up_a = phase([], *along_xy(cur_a))
    arrived = sum([nothing(item) for item in others])
    far_a = phase([], *across(right_a + arrived, up_a + arrived))
    arrived = nothing(far_a[0]) + nothing(far_a[1])
    cur_b = join(rest, [item + arrived for item in others])
    right_b, up_b = phase([], *along_xy(cur_b))
    (in0_full,) = put_together(place, [cur_a, right_a, up_a, *far_a], ((0,), PADDED))
    small = small_of(in0_full)
    arrived = nothing(small[0][0]).astype(LOW)
    near_right, near_up = right_b[:2] + arrived, up_b[2:] + arrived
    kept0 = forward(resid, in0_full, small[0], segs, near_right, near_up)
    arrived = nothing(kept0[3])
    far_b = [swap(near_right, 4, PARTS) + arrived, swap(near_up, 2, PARTS) + arrived]
    pieces = [cur_b, right_b, up_b, *far_b]
    start = 2 * WIDTH + PADDED
    out0_full, in1_full, out1_full = put_together(
        place, pieces, ((0, WIDTH), WIDTH), ((2 * WIDTH,), PADDED), ((start, start + WIDTH), WIDTH)
    )
    resid1 = project(resid, kept0[3], out0_full)
    kept1 = forward(resid1, in1_full, small[1], segs)
    mixed, grad = finish(project(resid1, kept1[3], out1_full), cotangent, segs)

    hidden, ssm, normed, gated = kept1
    gated_grad, keep, send = backward_out(place, grad, gated, out1_full)
    sum_c = Sums(keep)
    core = swap(send, 1, PARTS)
    dhidden, small1 = backward_mixer(gated_grad, hidden, ssm, small[1], segs)
    sum_c.add_core(core)

    to_far_c = sum_c.across()
    far_c = phase([], *to_far_c)
    grad, keep, send, gated_grad = backward_both(
        place, grad, resid1, normed, dhidden, in1_full, small[1][0], kept0[3], out0_full,
        *[item[0] for item in to_far_c],
    )
    sum_b = Sums(keep)

    hidden, ssm, normed, gated = kept0
    core = swap(send, 1, PARTS)
    to_xy_c = sum_c.along_xy(*far_c)
    got = phase([], *to_xy_c)
    dhidden, small0 = backward_mixer(
        gated_grad, hidden, ssm, small[0], segs, *[item[0] for item in to_xy_c]
    )
    sums = Total(small0, small1, me)
    sum_b.add_core(core)
    sum_c.add_xy(*got)

    to_far_b = sum_b.across()
    far_b = phase([], *to_far_b)
    (far_c,) = phase([], *sum_c.far_z())
    grad, keep, send = backward_in(
        place, grad, resid, normed, dhidden, in0_full, small[0][0], *[item[0] for item in to_far_b]
    )
    sum_a = Sums(keep)

    core = swap(send, 1, PARTS)
    to_xy = sum_b.along_xy(*far_b)
    right_b, up_b = phase([], *to_xy)
    (near_c,) = phase([], *sum_c.near_z(far_c))
    sums.add(8)
    sum_a.add_core(core)
    far_a = phase([], *sum_a.across())
    sums.add(16)
    to_xy = sum_a.along_xy(*far_a)
    sum_b.add_xy(right_b, up_b)
    right_a, up_a = phase([], *to_xy)
    (far_b,) = phase([], (sum_b.far_z()[0][0], 16))
    sum_a.add_xy(right_a, up_a)
    to_z = sum_a.along_z()
    parts = phase([], *to_z)
    sums.add(2, to_z[0][0])
    sums.add(4)
    (near_b,) = phase([], *sum_b.near_z(far_b))
    both = sum_b.end(near_b)
    in_grads = [sum_a.result(*parts), both[:, 2 * WIDTH :]]
    out_grads = [jnp.concatenate([both[:, :WIDTH], both[:, WIDTH : 2 * WIDTH]]), sum_c.end(near_c)]
    return mixed, grad, in_grads, out_grads, sums.both()


def body(
    count, tokens, segments, norm_gain, in_weight, conv_weight, conv_bias,
    log_decay, skip_gain, step_bias, gate_gain, out_weight, cotangent,
):
    layers, in_rows = in_weight.shape[:2]
    rows = tokens.shape[0] * BLOCK
    me = lax.axis_index("fsdp")
    chans, gates = conv_bias.shape[1], gate_gain.shape[1]
    packed = jnp.concatenate([norm_gain, conv_weight.reshape(layers, -1), conv_bias, gate_gain], axis=1)[None]
    padded = jnp.pad(in_weight, ((0, 0), (0, 0), (0, PADDED - PROJ)))
    segs = (segments.reshape(rows, 1), segments.reshape(1, rows))

    held = head_arrays(log_decay, skip_gain, step_bias)

    def small_of(packed):
        return small_arrays(packed, count, (in_rows, chans, gates), held)

    run = run_staged if count == PARTS and layers == 2 else partial(run_plain, count)
    mixed, grad, in_grads, out_grads, sums = run(
        me, tokens.reshape(rows, WIDTH).astype(F32), segs, cotangent.reshape(rows, WIDTH),
        [padded[layer] for layer in range(layers)], [out_weight[layer] for layer in range(layers)], packed, small_of,
    )
    total = sums

    def own(values, size):
        return lax.dynamic_slice_in_dim(values, me * size, size, axis=values.ndim - 1)

    by_head = total[:, 7, :INNER].reshape(layers, HEADS, HEADDIM).sum(axis=-1)
    return (
        mixed.reshape(tokens.shape),
        grad.reshape(tokens.shape),
        jnp.stack([item[:, PROJ] for item in in_grads]),
        jnp.stack([item[:, :PROJ] for item in in_grads]),
        own(total[:, 1 : 1 + CONV], chans),
        own(total[:, 5], chans),
        total[:, 0, :HEADS],
        by_head,
        total[:, 0, LANES : LANES + HEADS],
        own(total[:, 6, :INNER], gates),
        jnp.stack(out_grads),
    )


def solution(mesh):
    split0 = P("fsdp", None, None)
    split1 = P(None, "fsdp", None)
    in_specs = (
        split0, P("fsdp", None), P(None, "fsdp"), split1, P(None, None, "fsdp"), P(None, "fsdp"),
        P(), P(), P(), P(None, "fsdp"), split1, split0,
    )
    out_specs = (
        split0, split0, P(None, "fsdp"), split1, P(None, None, "fsdp"), P(None, "fsdp"),
        P(), P(), P(), P(None, "fsdp"), split1,
    )
    return jax.shard_map(
        partial(body, mesh.shape["fsdp"]), mesh=mesh, in_specs=in_specs, out_specs=out_specs, check_vma=False
    )
```
